32 devices in a mesh: ctx: 16 (over z, y, x), head: 2 (over core).
Axes of the slice: x: 2, y: 2, z: 4, core: 2. Of those that a mesh axis runs over, the one named last changes fastest.
Arguments:
- queries: bfloat16 [8192, 2048], P('ctx', 'head'), may hold values from -6 to 6
- key_vectors: bfloat16 [8192, 2048], P('ctx', 'head'), may hold values from -6 to 6
- values: bfloat16 [8192, 2048], P('ctx', 'head'), may hold values from -6 to 6
- level_table: float32 [64, 16, 7], P(None, 'head'), may hold values from 0.25 to 2
- weight_index: int32 [8192], P('ctx'), may hold values from 0 to 63
- norm_gain: float32 [2048], P('head'), may hold values from 0.25 to 1.75
- out_weight: bfloat16 [2048, 2048], P('head'), may hold values from -0.125 to 0.125
Outputs:
- mixed_out: bfloat16 [8192, 2048], P('ctx', 'head')
The draws below stay inside these ranges and needn't reach their ends.
All inputs are finite; a program needn't handle non-finite values.
Results may differ from the reference program's by a relative error of at most 0.01.
Values may be sent and summed in bfloat16 or wider, within the bound.
No kernel may reach another device: no remote copies, remote signals or barrier semaphores. Data moves between devices by JAX's collectives and lax.ppermute only.
A program may use at most 128 MiB of HBM per device.

```python
import math
import jax
import jax.numpy as jnp
import numpy as np
from jax import lax

HEADS = 16
HEAD_DIM = 128
D = 2048
TOK_DEV = 512
STRETCHES_DEV = 4
STRETCH = 128
TABLE = 64
CTX_LEVELS = 4
LEVELS = 7
TOKENS = 8192
N_CTX = 16
N_HEAD = 2


def place_ends(entries, key, low, largest):
    spot = [jax.random.randint(jax.random.fold_in(key, axis), (), 0, length) for axis, length in enumerate(entries.shape)]
    longest = entries.shape.index(max(entries.shape))
    neighbour = spot[:longest] + [(spot[longest] + 1) % entries.shape[longest]] + spot[longest + 1:]
    return entries.at[tuple(spot)].set(low).at[tuple(neighbour)].set(largest)


def level_of(own_key, dims, shards, low, top_value):
    def one(dim, blocks):
        draws = jax.random.uniform(jax.random.fold_in(jax.random.fold_in(own_key, 6), dim), (blocks,), jnp.float32, low / len(shards), top_value / len(shards))
        return jnp.repeat(jnp.exp(draws), dims[dim] // blocks).reshape((-1,) + (1,) * (len(dims) - dim - 1))

    level = one(*shards[0])
    for cut in shards[1:]:
        level = level * one(*cut)
    return level


def normal_values(rng, shape, width, reach, split=(), kind=jnp.bfloat16):
    array = width * jax.random.normal(rng, shape, jnp.float32)
    if split:
        array = array * level_of(rng, shape, split, -0.22, 0.18)
    return jnp.clip(array, -reach, reach).astype(kind)


def setup_inputs(seed: int = 0) -> dict:
    key_list = jax.random.split(jax.random.key(seed), 8)
    return {
        "queries": normal_values(key_list[0], (TOKENS, D), 1.0, 6.0, ((0, 16), (1, 2))),
        "key_vectors": normal_values(key_list[1], (TOKENS, D), 1.0, 6.0, ((0, 16), (1, 2))),
        "values": normal_values(key_list[2], (TOKENS, D), 1.0, 6.0, ((0, 16), (1, 2))),
        "level_table": jnp.clip(jnp.exp(math.log(2.0) - 2.0794415 * jax.random.uniform(key_list[3], (TABLE, HEADS, LEVELS), jnp.float32) ** level_of(key_list[3], (TABLE, HEADS, LEVELS), ((1, 2),), -0.2, 0.2)), 0.25, 2.0),
        "weight_index": place_ends(jax.random.randint(key_list[4], (TOKENS,), 0, TABLE), jax.random.fold_in(key_list[4], 1), 0, TABLE - 1).astype(jnp.int32),
        "norm_gain": jnp.clip(1.0 + 0.15 * jax.random.normal(key_list[5], (D,), jnp.float32), 0.25, 1.75),
        "out_weight": normal_values(key_list[6], (D, D), D ** -0.5, 0.125, ((0, 2),)),
    }


ROPE_BASE = 500000.0
NORM_EPS = 1e-06

def rotate(vectors, positions):
    half_dim = vectors.shape[-1] // 2
    frequency = jnp.exp(jnp.arange(half_dim, dtype=jnp.float32) * (-2.0 * math.log(ROPE_BASE) / vectors.shape[-1]))
    angles = positions[:, None] * frequency[None, :]
    cosine = jnp.cos(angles)[:, None, :]
    sine_part = jnp.sin(angles)[:, None, :]
    widened = vectors.astype(jnp.float32)
    leading = widened[..., :half_dim]
    trailing = widened[..., half_dim:]
    turned = jnp.concatenate([leading * cosine - trailing * sine_part, trailing * cosine + leading * sine_part], axis=-1)
    return turned.astype(jnp.bfloat16)

def level_scale(level_index, stretch_len):
    if level_index == 0:
        return stretch_len ** (-0.5)
    return (2 ** (level_index - 1) * stretch_len) ** (-0.5)

def rounded(matrix):
    return lax.optimization_barrier(matrix.astype(jnp.bfloat16)).astype(jnp.float32)

def local_buckets(states):
    stretch_count = states.shape[0]
    stretch_ids = np.arange(stretch_count)
    result = []
    for bit_index in range(stretch_count.bit_length() - 1):
        grouped = states.reshape((stretch_count >> bit_index, 1 << bit_index) + states.shape[1:]).sum(axis=1)
        source = np.maximum((stretch_ids >> bit_index) - 1, 0)
        present = stretch_ids >> bit_index & 1 == 1
        result.append(jnp.where(jnp.asarray(present)[:, None, None, None], grouped[source], 0.0))
    return result

def shard_pieces(start, queries, key_vectors, values):
    positions = (start + jnp.arange(TOK_DEV, dtype=jnp.int32)).astype(jnp.float32)
    query_block = lax.dynamic_slice_in_dim(queries, start, TOK_DEV, 0).reshape(TOK_DEV, HEADS, HEAD_DIM)
    key_block = lax.dynamic_slice_in_dim(key_vectors, start, TOK_DEV, 0).reshape(TOK_DEV, HEADS, HEAD_DIM)
    value_block = lax.dynamic_slice_in_dim(values, start, TOK_DEV, 0).reshape(TOK_DEV, HEADS, HEAD_DIM)
    return (rotate(query_block, positions), rotate(key_block, positions), value_block)

def stretch_states(rotated_keys, value_block):
    key_stretches = rotated_keys.reshape(STRETCHES_DEV, STRETCH, HEADS, HEAD_DIM).astype(jnp.float32)
    value_stretches = value_block.reshape(STRETCHES_DEV, STRETCH, HEADS, HEAD_DIM).astype(jnp.float32)
    return jnp.einsum('cthd,cthe->chde', key_stretches, value_stretches, precision=lax.Precision.HIGHEST)

def reference(queries, key_vectors, values, level_table, weight_index, norm_gain, out_weight):
    starts = jnp.arange(N_CTX, dtype=jnp.int32) * TOK_DEV

    def shard_total(start):
        rotated_queries, rotated_keys, value_block = shard_pieces(start, queries, key_vectors, values)
        return stretch_states(rotated_keys, value_block).sum(axis=0)
    shard_states = lax.map(shard_total, starts)
    grouped_levels = [shard_states.reshape((N_CTX >> bit_index, 1 << bit_index) + shard_states.shape[1:]).sum(axis=1) for bit_index in range(CTX_LEVELS)]

    def shard_output(shard_index):
        start = shard_index * TOK_DEV
        rotated_queries, rotated_keys, value_block = shard_pieces(start, queries, key_vectors, values)
        states = stretch_states(rotated_keys, value_block)
        query_stretches = rotated_queries.reshape(STRETCHES_DEV, STRETCH, HEADS, HEAD_DIM).astype(jnp.float32)
        key_stretches = rotated_keys.reshape(STRETCHES_DEV, STRETCH, HEADS, HEAD_DIM).astype(jnp.float32)
        value_stretches = value_block.reshape(STRETCHES_DEV, STRETCH, HEADS, HEAD_DIM).astype(jnp.float32)
        scores = jnp.einsum('cthd,cshd->chts', query_stretches, key_stretches, precision=lax.Precision.HIGHEST)
        causal_mask = jnp.tril(jnp.ones((STRETCH, STRETCH), dtype=bool))
        scores = jnp.where(causal_mask, scores, 0.0).astype(jnp.bfloat16)
        level_outs = [jnp.einsum('chts,cshe->cthe', scores.astype(jnp.float32), value_stretches, precision=lax.Precision.HIGHEST).reshape(TOK_DEV, HEADS, HEAD_DIM)]
        for bucket in local_buckets(states):
            level_outs.append(jnp.einsum('cthd,chde->cthe', query_stretches, rounded(bucket), precision=lax.Precision.HIGHEST).reshape(TOK_DEV, HEADS, HEAD_DIM))
        query_wide = rotated_queries.astype(jnp.float32)
        for bit_index in range(CTX_LEVELS):
            position = jnp.maximum((shard_index >> bit_index) - 1, 0).astype(jnp.int32)
            present = (shard_index >> bit_index & 1).astype(jnp.float32)
            bucket = lax.dynamic_index_in_dim(grouped_levels[bit_index], position, 0, keepdims=False) * present
            level_outs.append(jnp.einsum('thd,hde->the', query_wide, rounded(bucket), precision=lax.Precision.HIGHEST))
        table_rows = lax.dynamic_slice_in_dim(weight_index, start, TOK_DEV, 0)
        level_weights = level_table[table_rows]
        combined = jnp.zeros((TOK_DEV, HEADS, HEAD_DIM), jnp.float32)
        for level_index in range(len(level_outs)):
            combined = combined + level_weights[:, :, level_index, None] * level_scale(level_index, STRETCH) * level_outs[level_index]
        mean_square = lax.optimization_barrier(jnp.mean(combined * combined, axis=-1, keepdims=True))
        normed = combined * lax.rsqrt(mean_square + NORM_EPS) * norm_gain.reshape(HEADS, HEAD_DIM)
        hidden = normed.astype(jnp.bfloat16).reshape(TOK_DEV, D)
        group_width = D // N_HEAD
        total = jnp.zeros((TOK_DEV, D), jnp.float32)
        for group in range(N_HEAD):
            part_rows = hidden[:, group * group_width:(group + 1) * group_width]
            weight_rows = out_weight[group * group_width:(group + 1) * group_width]
            total = total + rounded(jnp.dot(part_rows, weight_rows, preferred_element_type=jnp.float32))
        return total.astype(jnp.bfloat16)
    output_rows = lax.map(shard_output, jnp.arange(N_CTX, dtype=jnp.int32))
    return output_rows.reshape(TOKENS, D)
```

```python
import functools
import math

import jax
import jax.numpy as jnp
import numpy as np
from jax import lax
from jax.experimental import pallas as pl
from jax.experimental.pallas import tpu as pltpu
from jax.sharding import PartitionSpec as P

STRETCHES_DEV = 4
ROPE_BASE = 500000.0
NORM_EPS = 1e-06
MIB = 1 << 20

F32 = jnp.float32
BF16 = jnp.bfloat16


def angle_tables(positions, head_dim):
    half_dim = head_dim // 2
    frequency = np.exp(np.arange(half_dim) * (-2.0 * math.log(ROPE_BASE) / head_dim))
    angles = np.asarray(positions, np.float64)[:, None] * frequency[None, :]
    cosine, sine = np.cos(angles), np.sin(angles)
    return (
        np.concatenate([cosine, cosine], axis=1).astype(np.float32),
        np.concatenate([-sine, sine], axis=1).astype(np.float32),
    )


def level_scale(level_index, stretch_len):
    if level_index == 0:
        return stretch_len ** (-0.5)
    return (2 ** (level_index - 1) * stretch_len) ** (-0.5)


def fill_angles(row_cos_ref, row_sin_ref, base_ref, cos_ref, sin_ref):
    base_cos = base_ref[0:1, :]
    base_sin = base_ref[1:2, :]
    row_cos = row_cos_ref[...]
    row_sin = row_sin_ref[...]
    cos_ref[...] = base_cos * row_cos - base_sin * row_sin
    sin_ref[...] = base_sin * row_cos + base_cos * row_sin


def rotated(vectors, cosine, sine):
    wide = vectors.astype(F32)
    half = wide.shape[-1] // 2
    return (wide * cosine + pltpu.roll(wide, half, 1) * sine).astype(BF16)


def dot_tn(a, b):
    return lax.dot_general(a, b, (((0,), (0,)), ((), ())), preferred_element_type=F32)


def dot_nt(a, b):
    return lax.dot_general(a, b, (((1,), (1,)), ((), ())), preferred_element_type=F32)


def dot_nn(a, b):
    return jnp.dot(a, b, preferred_element_type=F32)


def local_plan(stretches):
    plan = []
    for stretch in range(stretches):
        row = []
        for bit in range(stretches.bit_length() - 1):
            if stretch >> bit & 1:
                end = stretch >> bit << bit
                row.append((bit, tuple(range(end - (1 << bit), end))))
        plan.append(row)
    return plan


def state_kernel(
    heads_step,
    head_dim,
    row_cos_ref,
    row_sin_ref,
    base_ref,
    key_ref,
    value_ref,
    key_out,
    total_out,
    bucket_out,
    cos_ref,
    sin_ref,
):
    @pl.when(pl.program_id(0) == 0)
    def _():
        fill_angles(row_cos_ref, row_sin_ref, base_ref, cos_ref, sin_ref)

    tok_rows = key_ref.shape[0]
    stretch_len = tok_rows // STRETCHES_DEV
    groups = bucket_groups()
    for head in range(heads_step):
        cols = slice(head * head_dim, (head + 1) * head_dim)
        states = []
        for stretch in range(STRETCHES_DEV):
            rows = slice(stretch * stretch_len, (stretch + 1) * stretch_len)
            turned = rotated(key_ref[rows, cols], cos_ref[rows, :], sin_ref[rows, :])
            key_out[rows, cols] = turned
            states.append(dot_tn(turned, value_ref[rows, cols]))
        for spot, members in enumerate(groups):
            bucket_out[head, spot] = sum(states[m] for m in members).astype(BF16)
        total_out[head] = sum(states).astype(BF16)


def bucket_groups():
    groups = []
    for row in local_plan(STRETCHES_DEV):
        for _, members in row:
            if members not in groups:
                groups.append(members)
    return groups


def fill_one_hot(index_ref, one_hot_ref):
    table_rows = one_hot_ref.shape[0] // 3
    rows = lax.broadcasted_iota(jnp.int32, one_hot_ref.shape, 0)
    rows = lax.rem(rows, table_rows)
    one_hot_ref[...] = jnp.where(rows == index_ref[...], 1.0, 0.0).astype(BF16)


def level_weights(one_hot_ref, table):
    high = table.astype(BF16)
    rest = table - high.astype(F32)
    middle = rest.astype(BF16)
    low = (rest - middle.astype(F32)).astype(BF16)
    return dot_tn(one_hot_ref[...], jnp.concatenate([high, middle, low], axis=0))


def local_kernel(
    heads_step,
    head_dim,
    row_cos_ref,
    row_sin_ref,
    base_ref,
    index_ref,
    table_ref,
    query_ref,
    key_ref,
    value_ref,
    bucket_ref,
    query_out,
    combined_out,
    weight_out,
    cos_ref,
    sin_ref,
    one_hot_ref,
):
    @pl.when(pl.program_id(0) == 0)
    def _():
        fill_angles(row_cos_ref, row_sin_ref, base_ref, cos_ref, sin_ref)
        fill_one_hot(index_ref, one_hot_ref)

    tok_rows = key_ref.shape[0]
    stretch_len = tok_rows // STRETCHES_DEV
    groups = bucket_groups()
    shape = (stretch_len, stretch_len)
    causal = lax.broadcasted_iota(jnp.int32, shape, 0) >= lax.broadcasted_iota(jnp.int32, shape, 1)
    for head in range(heads_step):
        cols = slice(head * head_dim, (head + 1) * head_dim)
        weights = level_weights(one_hot_ref, table_ref[head])
        weight_out[head] = weights
        for stretch, row in enumerate(local_plan(STRETCHES_DEV)):
            rows = slice(stretch * stretch_len, (stretch + 1) * stretch_len)
            turned = rotated(query_ref[rows, cols], cos_ref[rows, :], sin_ref[rows, :])
            query_out[rows, cols] = turned
            scores = jnp.where(causal, dot_nt(turned, key_ref[rows, cols]), 0.0).astype(BF16)
            total = weights[rows, 0:1] * dot_nn(scores, value_ref[rows, cols])
            for bit, members in row:
                read = dot_nn(turned, bucket_ref[head, groups.index(members)])
                total = total + weights[rows, bit + 1 : bit + 2] * read
            combined_out[rows, cols] = total


def cross_kernel(
    heads_step,
    head_dim,
    first_level,
    levels,
    present_ref,
    combined_ref,
    query_ref,
    weight_ref,
    gain_ref,
    *refs,
):
    bucket_refs = refs[:levels]
    hidden_out = refs[levels]
    for head in range(heads_step):
        cols = slice(head * head_dim, (head + 1) * head_dim)
        total = combined_ref[:, cols]
        queries = query_ref[:, cols]
        for level in range(levels):
            spot = first_level + level
            weight = weight_ref[head, :, spot : spot + 1] * present_ref[level]
            total = total + weight * dot_nn(queries, bucket_refs[level][head])
        mean_square = jnp.mean(total * total, axis=-1, keepdims=True)
        normed = total * lax.rsqrt(mean_square + NORM_EPS) * gain_ref[:, cols]
        hidden_out[:, cols] = normed.astype(BF16)


def project_kernel(place_ref, hidden_ref, weight_ref, out_ref):
    out_ref[...] = dot_nn(hidden_ref[...], weight_ref[...])


def project_add_kernel(place_ref, hidden_ref, weight_ref, part_ref, out_ref):
    out_ref[...] = (part_ref[...] + dot_nn(hidden_ref[...], weight_ref[...])).astype(BF16)


def cost(flops, size):
    return pl.CostEstimate(flops=int(flops), bytes_accessed=int(size), transcendentals=0)


def local(queries, key_vectors, values, level_table, weight_index, norm_gain, out_weight):
    tok_rows, model_width = queries.shape
    table_rows, heads_here, level_count = level_table.shape
    head_dim = model_width // heads_here
    stretch_len = tok_rows // STRETCHES_DEV
    n_ctx = lax.axis_size("ctx")
    n_head = lax.axis_size("head")
    ctx_bits = n_ctx.bit_length() - 1
    shard_index = lax.axis_index("ctx")
    head_index = lax.axis_index("head")
    group_count = len(bucket_groups())

    other_weight = lax.ppermute(out_weight, "head", [(i, i ^ 1) for i in range(n_head)])

    row_cos, row_sin = angle_tables(np.arange(tok_rows), head_dim)
    base_cos, base_sin = angle_tables(np.arange(n_ctx) * tok_rows, head_dim)
    base_all = jnp.asarray(np.stack([base_cos, base_sin], axis=1))
    base = lax.dynamic_index_in_dim(base_all, shard_index, 0, keepdims=False)

    step = 2
    steps = heads_here // step
    width = step * head_dim
    wide = pl.BlockSpec((tok_rows, width), lambda h: (0, h))
    table_spec = pl.BlockSpec((tok_rows, head_dim), lambda h: (0, 0))
    base_spec = pl.BlockSpec((2, head_dim), lambda h: (0, 0))
    state_spec = pl.BlockSpec((step, head_dim, head_dim), lambda h: (h, 0, 0))
    bucket_spec = pl.BlockSpec((step, group_count, head_dim, head_dim), lambda h: (h, 0, 0, 0))
    angle_scratch = [pltpu.VMEM((tok_rows, head_dim), F32)] * 2
    params = pltpu.CompilerParams(
        dimension_semantics=("arbitrary",), vmem_limit_bytes=32 * MIB
    )
    head_macs = tok_rows * head_dim * head_dim * heads_here
    block_bytes = tok_rows * model_width * 2

    keys, shard_state, local_states = pl.pallas_call(
        functools.partial(state_kernel, step, head_dim),
        grid=(steps,),
        in_specs=[table_spec, table_spec, base_spec, wide, wide],
        out_specs=[wide, state_spec, bucket_spec],
        out_shape=[
            jax.ShapeDtypeStruct((tok_rows, model_width), BF16),
            jax.ShapeDtypeStruct((heads_here, head_dim, head_dim), BF16),
            jax.ShapeDtypeStruct((heads_here, group_count, head_dim, head_dim), BF16),
        ],
        scratch_shapes=angle_scratch,
        compiler_params=params,
        cost_estimate=cost(2 * head_macs, 4 * block_bytes),
        name="states",
    )(row_cos, row_sin, base, key_vectors, values)

    scales = np.array([level_scale(i, stretch_len) for i in range(level_count)], np.float32)
    table = jnp.transpose(level_table, (1, 0, 2)) * scales

    rotated_queries, combined, weights = pl.pallas_call(
        functools.partial(local_kernel, step, head_dim),
        grid=(steps,),
        in_specs=[
            table_spec,
            table_spec,
            base_spec,
            pl.BlockSpec((1, tok_rows), lambda h: (0, 0)),
            pl.BlockSpec((step, table_rows, level_count), lambda h: (h, 0, 0)),
            wide,
            wide,
            wide,
            bucket_spec,
        ],
        out_specs=[
            wide,
            wide,
            pl.BlockSpec((step, tok_rows, level_count), lambda h: (h, 0, 0)),
        ],
        out_shape=[
            jax.ShapeDtypeStruct((tok_rows, model_width), BF16),
            jax.ShapeDtypeStruct((tok_rows, model_width), F32),
            jax.ShapeDtypeStruct((heads_here, tok_rows, level_count), F32),
        ],
        scratch_shapes=angle_scratch + [pltpu.VMEM((3 * table_rows, tok_rows), BF16)],
        compiler_params=params,
        cost_estimate=cost(8 * head_macs, 8 * block_bytes),
        name="local_levels",
    )(
        row_cos,
        row_sin,
        base,
        weight_index.reshape(1, tok_rows),
        table,
        queries,
        keys,
        values,
        local_states,
    )

    buckets = []
    running = shard_state
    for bit in range(ctx_bits):
        partner = lax.ppermute(running, "ctx", [(i, i ^ (1 << bit)) for i in range(n_ctx)])
        buckets.append(partner)
        running = (running.astype(F32) + partner.astype(F32)).astype(BF16)
    present = (shard_index >> jnp.arange(ctx_bits, dtype=jnp.int32) & 1).astype(F32)

    first_cross = level_count - ctx_bits

    hidden = pl.pallas_call(
        functools.partial(cross_kernel, step, head_dim, first_cross, ctx_bits),
        grid=(steps,),
        in_specs=[
            pl.BlockSpec(memory_space=pltpu.SMEM),
            wide,
            wide,
            pl.BlockSpec((step, tok_rows, level_count), lambda h: (h, 0, 0)),
            pl.BlockSpec((1, width), lambda h: (0, h)),
        ]
        + [state_spec] * ctx_bits,
        out_specs=wide,
        out_shape=jax.ShapeDtypeStruct((tok_rows, model_width), BF16),
        compiler_params=params,
        cost_estimate=cost(2 * ctx_bits * head_macs, 6 * block_bytes),
        name="cross_levels",
    )(present, combined, rotated_queries, weights, norm_gain.reshape(1, model_width), *buckets)

    other_hidden = lax.ppermute(hidden, "head", [(i, i ^ 1) for i in range(n_head)])

    out_cols = out_weight.shape[1] // n_head
    tile = min(512, out_cols)
    tiles = out_cols // tile
    place = (head_index * tiles).astype(jnp.int32).reshape(1)
    hidden_spec = pl.BlockSpec((tok_rows, model_width), lambda n, place: (0, 0))
    weight_spec = pl.BlockSpec((model_width, tile), lambda n, place: (0, place[0] + n))
    out_spec = pl.BlockSpec((tok_rows, tile), lambda n, place: (0, n))
    matmul_flops = 2 * tok_rows * model_width * out_cols

    own_part = pl.pallas_call(
        project_kernel,
        grid_spec=pltpu.PrefetchScalarGridSpec(
            num_scalar_prefetch=1,
            grid=(tiles,),
            in_specs=[hidden_spec, weight_spec],
            out_specs=out_spec,
        ),
        out_shape=jax.ShapeDtypeStruct((tok_rows, out_cols), F32),
        compiler_params=params,
        cost_estimate=cost(matmul_flops, 8 * MIB),
        name="own_group",
    )(place, hidden, out_weight)

    return pl.pallas_call(
        project_add_kernel,
        grid_spec=pltpu.PrefetchScalarGridSpec(
            num_scalar_prefetch=1,
            grid=(tiles,),
            in_specs=[hidden_spec, weight_spec, out_spec],
            out_specs=out_spec,
        ),
        out_shape=jax.ShapeDtypeStruct((tok_rows, out_cols), BF16),
        compiler_params=params,
        cost_estimate=cost(matmul_flops, 8 * MIB),
        name="other_group",
    )(place, other_hidden, other_weight, own_part)


def solution(mesh):
    return jax.shard_map(
        local,
        mesh=mesh,
        in_specs=(
            P("ctx", "head"),
            P("ctx", "head"),
            P("ctx", "head"),
            P(None, "head", None),
            P("ctx"),
            P("head"),
            P("head", None),
        ),
        out_specs=P("ctx", "head"),
        check_vma=False,
    )
```

```python
import functools
import math

import jax
import jax.numpy as jnp
import numpy as np
from jax import lax
from jax.experimental import pallas as pl
from jax.experimental.pallas import tpu as pltpu
from jax.sharding import PartitionSpec as P

STRETCHES_DEV = 4
ROPE_BASE = 500000.0
NORM_EPS = 1e-06
VMEM_LIMIT = 56 << 20

F32 = jnp.float32
BF16 = jnp.bfloat16


def angle_tables(positions, head_dim):
    half_dim = head_dim // 2
    frequency = np.exp(np.arange(half_dim) * (-2.0 * math.log(ROPE_BASE) / head_dim))
    angles = np.asarray(positions, np.float64)[:, None] * frequency[None, :]
    cosine, sine = np.cos(angles), np.sin(angles)
    return (
        np.concatenate([cosine, cosine], axis=1).astype(np.float32),
        np.concatenate([-sine, sine], axis=1).astype(np.float32),
    )


def level_scale(level_index, stretch_len):
    if level_index == 0:
        return stretch_len ** (-0.5)
    return (2 ** (level_index - 1) * stretch_len) ** (-0.5)


def fill_angles(row_cos_ref, row_sin_ref, base_ref, cos_ref, sin_ref):
    base_cos = base_ref[0:1, :]
    base_sin = base_ref[1:2, :]
    row_cos = row_cos_ref[...]
    row_sin = row_sin_ref[...]
    cos_ref[...] = base_cos * row_cos - base_sin * row_sin
    sin_ref[...] = base_sin * row_cos + base_cos * row_sin


def rotated(vectors, cosine, sine):
    wide = vectors.astype(F32)
    half = wide.shape[-1] // 2
    return (wide * cosine + pltpu.roll(wide, half, 1) * sine).astype(BF16)


def dot_tn(a, b):
    return lax.dot_general(a, b, (((0,), (0,)), ((), ())), preferred_element_type=F32)


def dot_nt(a, b):
    return lax.dot_general(a, b, (((1,), (1,)), ((), ())), preferred_element_type=F32)


def dot_nn(a, b):
    return jnp.dot(a, b, preferred_element_type=F32)


def local_plan(stretches):
    plan = []
    for stretch in range(stretches):
        row = []
        for bit in range(stretches.bit_length() - 1):
            if stretch >> bit & 1:
                end = stretch >> bit << bit
                row.append((bit, tuple(range(end - (1 << bit), end))))
        plan.append(row)
    return plan


def state_kernel(
    slots,
    quarter_heads,
    head_dim,
    place_ref,
    row_cos_ref,
    row_sin_ref,
    base_ref,
    key_ref,
    value_ref,
    key_out,
    bucket_out,
    *refs,
):
    total_outs = refs[:slots]
    cos_ref, sin_ref = refs[slots:]
    slot = pl.program_id(0)

    @pl.when(slot == 0)
    def _():
        fill_angles(row_cos_ref, row_sin_ref, base_ref, cos_ref, sin_ref)

    tok_rows = key_ref.shape[0]
    stretch_len = tok_rows // STRETCHES_DEV
    groups = bucket_groups()
    for head in range(quarter_heads):
        cols = slice(head * head_dim, (head + 1) * head_dim)
        states = []
        for stretch in range(STRETCHES_DEV):
            rows = slice(stretch * stretch_len, (stretch + 1) * stretch_len)
            turned = rotated(key_ref[rows, cols], cos_ref[rows, :], sin_ref[rows, :])
            key_out[rows, cols] = turned
            states.append(dot_tn(turned, value_ref[rows, cols]))
        for spot, members in enumerate(groups):
            bucket_out[head, spot] = sum(states[m] for m in members).astype(BF16)
        total = sum(states).astype(BF16)
        for index in range(slots):

            @pl.when(slot == index)
            def _():
                total_outs[index][head] = total


def bucket_groups():
    groups = []
    for row in local_plan(STRETCHES_DEV):
        for _, members in row:
            if members not in groups:
                groups.append(members)
    return groups


def fill_one_hot(index_ref, one_hot_ref):
    table_rows = one_hot_ref.shape[0] // 3
    rows = lax.broadcasted_iota(jnp.int32, one_hot_ref.shape, 0)
    rows = lax.rem(rows, table_rows)
    one_hot_ref[...] = jnp.where(rows == index_ref[...], 1.0, 0.0).astype(BF16)


def level_weights(one_hot_ref, table):
    high = table.astype(BF16)
    rest = table - high.astype(F32)
    middle = rest.astype(BF16)
    low = (rest - middle.astype(F32)).astype(BF16)
    return dot_tn(one_hot_ref[...], jnp.concatenate([high, middle, low], axis=0))


def local_kernel(
    quarter_heads,
    head_dim,
    first_slot,
    place_ref,
    row_cos_ref,
    row_sin_ref,
    base_ref,
    index_ref,
    table_ref,
    scale_ref,
    query_ref,
    key_ref,
    value_ref,
    bucket_ref,
    query_out,
    combined_out,
    weight_out,
    cos_ref,
    sin_ref,
    one_hot_ref,
):
    @pl.when(pl.program_id(0) == 0)
    def _():
        fill_angles(row_cos_ref, row_sin_ref, base_ref, cos_ref, sin_ref)
        fill_one_hot(index_ref, one_hot_ref)

    tok_rows = key_ref.shape[0]
    levels = scale_ref.shape[1]
    stretch_len = tok_rows // STRETCHES_DEV
    groups = bucket_groups()
    shape = (stretch_len, stretch_len)
    causal = lax.broadcasted_iota(jnp.int32, shape, 0) >= lax.broadcasted_iota(jnp.int32, shape, 1)
    quarter = place_ref[first_slot + pl.program_id(0)]
    for head in range(quarter_heads):
        cols = slice(head * head_dim, (head + 1) * head_dim)
        table = table_ref[:, pl.ds(quarter * quarter_heads + head, 1), :]
        table = table.reshape(table.shape[0], levels) * scale_ref[...]
        weights = level_weights(one_hot_ref, table)
        weight_out[0, :, head * levels : (head + 1) * levels] = weights
        for stretch, row in enumerate(local_plan(STRETCHES_DEV)):
            rows = slice(stretch * stretch_len, (stretch + 1) * stretch_len)
            turned = rotated(query_ref[rows, cols], cos_ref[rows, :], sin_ref[rows, :])
            query_out[rows, cols] = turned
            scores = jnp.where(causal, dot_nt(turned, key_ref[rows, cols]), 0.0).astype(BF16)
            total = weights[rows, 0:1] * dot_nn(scores, value_ref[rows, cols])
            for bit, members in row:
                read = dot_nn(turned, bucket_ref[head, groups.index(members)])
                total = total + weights[rows, bit + 1 : bit + 2] * read
            combined_out[rows, cols] = total


def cross_kernel(
    slots,
    quarter_heads,
    head_dim,
    levels,
    low_levels,
    high_levels,
    place_ref,
    combined_ref,
    query_ref,
    weight_ref,
    gain_ref,
    *refs,
):
    low_refs = refs[:slots]
    high_refs = refs[slots : 2 * slots]
    hidden_out = refs[2 * slots]
    shard_index = place_ref[place_ref.shape[0] - 2]
    cross_levels = low_levels + high_levels
    present = [(shard_index >> bit & 1).astype(F32) for bit in range(cross_levels)]
    for slot in range(slots):

        @pl.when(pl.program_id(0) == slot)
        def _():
            for head in range(quarter_heads):
                cols = slice(head * head_dim, (head + 1) * head_dim)
                total = combined_ref[:, cols]
                queries = query_ref[:, cols]
                for level in range(cross_levels):
                    if level < low_levels:
                        bucket = low_refs[slot][level * quarter_heads + head]
                    else:
                        bucket = high_refs[slot][(level - low_levels) * quarter_heads + head]
                    spot = head * levels + levels - cross_levels + level
                    weight = weight_ref[0, :, spot : spot + 1] * present[level]
                    total = total + weight * dot_nn(queries, bucket)
                mean_square = jnp.mean(total * total, axis=-1, keepdims=True)
                normed = total * lax.rsqrt(mean_square + NORM_EPS) * gain_ref[:, cols]
                hidden_out[:, cols] = normed.astype(BF16)


def project(slots, place_ref, hidden_refs, weight_ref):
    width = weight_ref.shape[0] // slots
    here = slots // len(hidden_refs)
    total = None
    for slot in range(slots):
        start = pl.multiple_of(place_ref[slot] * width, width)
        spot = slot % here * width
        part = dot_nn(
            hidden_refs[slot // here][:, spot : spot + width], weight_ref[pl.ds(start, width), :]
        )
        total = part if total is None else total + part
    return total


def own_kernel(slots, place_ref, *refs):
    *hidden_refs, weight_ref, out_ref = refs
    out_ref[...] = project(slots, place_ref, hidden_refs, weight_ref).astype(BF16)


def other_kernel(slots, place_ref, *refs):
    *hidden_refs, weight_ref, part_ref, out_ref = refs
    total = project(slots, place_ref, hidden_refs, weight_ref).astype(BF16).astype(F32)
    out_ref[...] = (part_ref[...].astype(F32) + total).astype(BF16)


def cost(flops, size):
    return pl.CostEstimate(flops=int(flops), bytes_accessed=int(size), transcendentals=0)


def bfloat_sum(*blocks):
    return sum(block.astype(F32) for block in blocks).astype(BF16)


def high_buckets(total, shard_index, first_bit, ctx_bits, n_ctx):
    buckets = []
    for low in range(first_bit, ctx_bits, 2):
        bits = min(2, ctx_bits - low)
        radix = 1 << bits
        mask = (radix - 1) << low
        digit = shard_index >> low & (radix - 1)

        def turned(index, by):
            return index & ~mask | (((index >> low) + by) & (radix - 1)) << low

        back = [
            lax.ppermute(total, "ctx", [(i, turned(i, by)) for i in range(n_ctx)])
            for by in range(1, radix)
        ]
        buckets.append(back[0])
        if bits == 2:
            wide = [block.astype(F32) for block in back]
            buckets.append(
                jnp.where(digit == 2, wide[0] + wide[1], wide[1] + wide[2]).astype(BF16)
            )
        if low + bits < ctx_bits:
            total = bfloat_sum(total, *back)
    return buckets


def local(queries, key_vectors, values, level_table, weight_index, norm_gain, out_weight):
    tok_rows, model_width = queries.shape
    table_rows, heads_here, level_count = level_table.shape
    head_dim = model_width // heads_here
    stretch_len = tok_rows // STRETCHES_DEV
    n_ctx = lax.axis_size("ctx")
    n_head = lax.axis_size("head")
    ctx_bits = n_ctx.bit_length() - 1
    shard_index = lax.axis_index("ctx")
    head_index = lax.axis_index("head")
    group_count = len(bucket_groups())

    low_bits = min(2, ctx_bits)
    slots = 1 << low_bits
    quarter_heads = heads_here // slots
    width = quarter_heads * head_dim
    chunk = slots // 2

    def swap_heads(block):
        return lax.ppermute(block, "head", [(i, i ^ 1) for i in range(n_head)])

    def swap_low(block, by):
        return lax.ppermute(block, "ctx", [(i, i ^ by) for i in range(n_ctx)])

    other_weight = swap_heads(out_weight)
    order = jnp.arange(slots, dtype=jnp.int32) ^ (shard_index & (slots - 1)).astype(jnp.int32)
    place = jnp.concatenate(
        [order, jnp.stack([shard_index, head_index]).astype(jnp.int32)]
    )

    row_cos, row_sin = angle_tables(np.arange(tok_rows), head_dim)
    base = np.stack(angle_tables(np.arange(n_ctx) * tok_rows, head_dim), axis=1)
    scales = np.array([[level_scale(i, stretch_len) for i in range(level_count)]], np.float32)

    def fixed(*shape):
        return pl.BlockSpec(shape, lambda s, place: (0,) * len(shape))

    def ordered(first):
        return pl.BlockSpec((tok_rows, width), lambda s, place: (0, place[first + s]))

    def by_slot(first):
        return pl.BlockSpec((tok_rows, width), lambda s, place: (0, first + s))

    def bucket_by_slot(first):
        return pl.BlockSpec(
            (quarter_heads, group_count, head_dim, head_dim), lambda s, place: (first + s, 0, 0, 0)
        )

    angle_specs = [
        fixed(tok_rows, head_dim),
        fixed(tok_rows, head_dim),
        pl.BlockSpec((None, 2, head_dim), lambda s, place: (place[slots], 0, 0)),
    ]
    angle_scratch = [pltpu.VMEM((tok_rows, head_dim), F32)] * 2
    params = pltpu.CompilerParams(
        dimension_semantics=("arbitrary",), vmem_limit_bytes=VMEM_LIMIT
    )
    head_macs = tok_rows * head_dim * head_dim * heads_here
    block_bytes = tok_rows * model_width * 2

    keys, local_states, *shares = pl.pallas_call(
        functools.partial(state_kernel, slots, quarter_heads, head_dim),
        grid_spec=pltpu.PrefetchScalarGridSpec(
            num_scalar_prefetch=1,
            grid=(slots,),
            in_specs=angle_specs + [ordered(0), ordered(0)],
            out_specs=[by_slot(0), bucket_by_slot(0)]
            + [fixed(quarter_heads, head_dim, head_dim)] * slots,
            scratch_shapes=angle_scratch,
        ),
        out_shape=[
            jax.ShapeDtypeStruct((tok_rows, model_width), BF16),
            jax.ShapeDtypeStruct((heads_here, group_count, head_dim, head_dim), BF16),
        ]
        + [jax.ShapeDtypeStruct((quarter_heads, head_dim, head_dim), BF16)] * slots,
        compiler_params=params,
        cost_estimate=cost(2 * head_macs, 4 * block_bytes),
        name="states",
    )(place, row_cos, row_sin, base, key_vectors, values)

    def local_levels(first):
        return pl.pallas_call(
            functools.partial(local_kernel, quarter_heads, head_dim, first),
            grid_spec=pltpu.PrefetchScalarGridSpec(
                num_scalar_prefetch=1,
                grid=(chunk,),
                in_specs=angle_specs
                + [
                    fixed(1, tok_rows),
                    fixed(table_rows, heads_here, level_count),
                    fixed(1, level_count),
                    ordered(first),
                    by_slot(first),
                    ordered(first),
                    bucket_by_slot(first),
                ],
                out_specs=[
                    by_slot(0),
                    by_slot(0),
                    pl.BlockSpec(
                        (1, tok_rows, quarter_heads * level_count), lambda s, place: (s, 0, 0)
                    ),
                ],
                scratch_shapes=angle_scratch + [pltpu.VMEM((3 * table_rows, tok_rows), BF16)],
            ),
            out_shape=[
                jax.ShapeDtypeStruct((tok_rows, chunk * width), BF16),
                jax.ShapeDtypeStruct((tok_rows, chunk * width), F32),
                jax.ShapeDtypeStruct((chunk, tok_rows, quarter_heads * level_count), F32),
            ],
            compiler_params=params,
            cost_estimate=cost(4 * head_macs, 4 * block_bytes),
            name="local_levels",
        )(
            place,
            row_cos,
            row_sin,
            base,
            weight_index.reshape(1, tok_rows),
            level_table,
            scales,
            queries,
            keys,
            values,
            local_states,
        )

    parts = [shares[0]] + [swap_low(shares[by], by) for by in range(1, slots)]
    total = bfloat_sum(*parts)

    def low_payload(by):
        levels = []
        for bit in range(low_bits):
            members = [m for m in range(slots) if m >> bit == 1]
            levels.append(bfloat_sum(*[parts[m ^ by] for m in members]))
        return jnp.concatenate(levels, axis=0)

    high = jnp.concatenate(high_buckets(total, shard_index, low_bits, ctx_bits, n_ctx), axis=0)
    low_slots = [low_payload(0)] + [swap_low(low_payload(by), by) for by in range(1, slots)]
    high_slots = [high] + [swap_low(high, by) for by in range(1, slots)]
    gain = norm_gain.reshape(1, model_width)
    high_bits = ctx_bits - low_bits

    hidden, other_hidden = [], []
    for first in range(0, slots, chunk):
        rotated_queries, combined, weights = local_levels(first)
        piece = pl.pallas_call(
            functools.partial(
                cross_kernel, chunk, quarter_heads, head_dim, level_count, low_bits, high_bits
            ),
            grid_spec=pltpu.PrefetchScalarGridSpec(
                num_scalar_prefetch=1,
                grid=(chunk,),
                in_specs=[
                    by_slot(0),
                    by_slot(0),
                    pl.BlockSpec(
                        (1, tok_rows, quarter_heads * level_count), lambda s, place: (s, 0, 0)
                    ),
                    pl.BlockSpec((1, width), lambda s, place, first=first: (0, place[first + s])),
                ]
                + [fixed(low_bits * quarter_heads, head_dim, head_dim)] * chunk
                + [fixed(high_bits * quarter_heads, head_dim, head_dim)] * chunk,
                out_specs=by_slot(0),
            ),
            out_shape=jax.ShapeDtypeStruct((tok_rows, chunk * width), BF16),
            compiler_params=params,
            cost_estimate=cost(ctx_bits * head_macs, 3 * block_bytes),
            name="cross_levels",
        )(
            place,
            combined,
            rotated_queries,
            weights,
            gain,
            *low_slots[first : first + chunk],
            *high_slots[first : first + chunk],
        )
        hidden.append(piece)
        other_hidden.append(swap_heads(piece))

    out_cols = out_weight.shape[1] // n_head
    tile = min(256, out_cols)
    tiles = out_cols // tile
    hidden_specs = [fixed(tok_rows, chunk * width)] * len(hidden)
    weight_spec = pl.BlockSpec(
        (model_width, tile), lambda n, place: (0, place[slots + 1] * tiles + n)
    )
    out_spec = pl.BlockSpec((tok_rows, tile), lambda n, place: (0, n))
    matmul_flops = 2 * tok_rows * model_width * out_cols

    def projection(kernel, name, in_specs, *operands):
        return pl.pallas_call(
            functools.partial(kernel, slots),
            grid_spec=pltpu.PrefetchScalarGridSpec(
                num_scalar_prefetch=1, grid=(tiles,), in_specs=in_specs, out_specs=out_spec
            ),
            out_shape=jax.ShapeDtypeStruct((tok_rows, out_cols), BF16),
            compiler_params=params,
            cost_estimate=cost(matmul_flops, 8 * block_bytes),
            name=name,
        )(place, *operands)

    own_part = projection(
        own_kernel, "own_group", hidden_specs + [weight_spec], *hidden, out_weight
    )
    return projection(
        other_kernel,
        "other_group",
        hidden_specs + [weight_spec, out_spec],
        *other_hidden,
        other_weight,
        own_part,
    )


def solution(mesh):
    return jax.shard_map(
        local,
        mesh=mesh,
        in_specs=(
            P("ctx", "head"),
            P("ctx", "head"),
            P("ctx", "head"),
            P(None, "head", None),
            P("ctx"),
            P("head"),
            P("head", None),
        ),
        out_specs=P("ctx", "head"),
        check_vma=False,
    )
```

```python
import functools
import math

import jax
import jax.numpy as jnp
import numpy as np
from jax import lax
from jax.experimental import pallas as pl
from jax.experimental.pallas import tpu as pltpu
from jax.sharding import PartitionSpec as P

STRETCHES_DEV = 4
ROPE_BASE = 500000.0
NORM_EPS = 1e-06
FETCH_LIMIT = 59 << 20
LOCAL_LIMIT = 40 << 20
SMALL_LIMIT = 20 << 20
FINE = 16

F32 = jnp.float32
BF16 = jnp.bfloat16


def angle_rows(positions, head_dim):
    half_dim = head_dim // 2
    frequency = np.exp(np.arange(half_dim) * (-2.0 * math.log(ROPE_BASE) / head_dim))
    angles = np.asarray(positions, np.float64)[:, None] * frequency[None, :]
    cosine, sine = np.cos(angles), np.sin(angles)
    return [
        np.concatenate([cosine, cosine], axis=1).astype(np.float32),
        np.concatenate([-sine, sine], axis=1).astype(np.float32),
    ]


def level_scale(level_index, stretch_len):
    if level_index == 0:
        return stretch_len ** (-0.5)
    return (2 ** (level_index - 1) * stretch_len) ** (-0.5)


def quarter_of(slot, slots):
    return slot ^ (lax.axis_index("ctx") & (slots - 1))


def turn_sum(cos_a, sin_a, cos_b, sin_b):
    return cos_a * cos_b - sin_a * sin_b, sin_a * cos_b + cos_a * sin_b


def fill_angles(angle_ref, shard_index, n_ctx, cos_ref, sin_ref):
    coarse = cos_ref.shape[0] // FINE
    fine_cos, fine_sin = angle_ref[0:FINE, :], angle_ref[FINE : 2 * FINE, :]
    first = 2 * FINE
    coarse_cos = angle_ref[first : first + coarse, :]
    coarse_sin = angle_ref[first + coarse : first + 2 * coarse, :]
    first += 2 * coarse
    base_cos = angle_ref[pl.ds(first + shard_index, 1), :]
    base_sin = angle_ref[pl.ds(first + n_ctx + shard_index, 1), :]
    coarse_cos, coarse_sin = turn_sum(coarse_cos, coarse_sin, base_cos, base_sin)
    for index in range(coarse):
        rows = slice(index * FINE, (index + 1) * FINE)
        cos_ref[rows, :], sin_ref[rows, :] = turn_sum(
            coarse_cos[index : index + 1, :], coarse_sin[index : index + 1, :], fine_cos, fine_sin
        )


def rotated(vectors, cosine, sine):
    wide = vectors.astype(F32)
    half = wide.shape[-1] // 2
    return (wide * cosine + pltpu.roll(wide, half, 1) * sine).astype(BF16)


def dot_tn(a, b):
    return lax.dot_general(a, b, (((0,), (0,)), ((), ())), preferred_element_type=F32)


def dot_nt(a, b):
    return lax.dot_general(a, b, (((1,), (1,)), ((), ())), preferred_element_type=F32)


def dot_nn(a, b):
    return jnp.dot(a, b, preferred_element_type=F32)


def local_plan(stretches):
    plan = []
    for stretch in range(stretches):
        row = []
        for bit in range(stretches.bit_length() - 1):
            if stretch >> bit & 1:
                end = stretch >> bit << bit
                row.append((bit, tuple(range(end - (1 << bit), end))))
        plan.append(row)
    return plan


def state_kernel(
    slots,
    head_dim,
    n_ctx,
    angle_hbm,
    query_hbm,
    key_hbm,
    value_hbm,
    query_out,
    value_out,
    key_out,
    cos_out,
    sin_out,
    bucket_out,
    *refs,
):
    total_outs = refs[:slots]
    key_raw, angle_ref, sems = refs[slots:]
    tok_rows, model_width = key_raw.shape
    width = model_width // slots

    def fetch(source, target, slot, sem):
        start = pl.multiple_of(quarter_of(slot, slots) * width, width)
        return pltpu.make_async_copy(
            source.at[:, pl.ds(start, width)], target.at[:, pl.ds(slot * width, width)], sem
        )

    angles_in = pltpu.make_async_copy(angle_hbm, angle_ref, sems.at[3, 0])
    angles_in.start()
    order = list(range(slots - 1, -1, -1))
    copies = {}
    for kind, (source, target) in enumerate(
        ((key_hbm, key_raw), (value_hbm, value_out), (query_hbm, query_out))
    ):
        for slot in order:
            copies[kind, slot] = fetch(source, target, slot, sems.at[kind, slot])
    for slot in order:
        copies[0, slot].start()
        copies[1, slot].start()
    for slot in range(slots):
        copies[2, slot].start()
    angles_in.wait()
    fill_angles(angle_ref, lax.axis_index("ctx"), n_ctx, cos_out, sin_out)

    stretch_len = tok_rows // STRETCHES_DEV
    groups = bucket_groups()
    quarter_heads = width // head_dim
    for slot in order:
        copies[0, slot].wait()
        copies[1, slot].wait()
        heads = range(slot * quarter_heads, (slot + 1) * quarter_heads)
        turned, states = {}, {}
        for head in heads:
            cols = slice(head * head_dim, (head + 1) * head_dim)
            for stretch in range(STRETCHES_DEV):
                rows = slice(stretch * stretch_len, (stretch + 1) * stretch_len)
                block = rotated(key_raw[rows, cols], cos_out[rows, :], sin_out[rows, :])
                turned[head, stretch] = block
                states[head, stretch] = dot_tn(block, value_out[rows, cols])
        for head in heads:
            cols = slice(head * head_dim, (head + 1) * head_dim)
            for stretch in range(STRETCHES_DEV):
                rows = slice(stretch * stretch_len, (stretch + 1) * stretch_len)
                key_out[rows, cols] = turned[head, stretch]
            sums = {}
            for group, members in enumerate(groups):
                sums[members] = sum(states[head, m] for m in members)
                bucket_out[head, group] = sums[members].astype(BF16)
            total = sum(states[head, m] for m in range(STRETCHES_DEV))
            total_outs[slot][head - heads[0]] = total.astype(BF16)
    for slot in range(slots):
        copies[2, slot].wait()


def bucket_groups():
    groups = []
    for row in local_plan(STRETCHES_DEV):
        for _, members in row:
            if members not in groups:
                groups.append(members)
    return groups


def fill_one_hot(index_ref, one_hot_ref):
    table_rows = one_hot_ref.shape[0] // 3
    rows = lax.broadcasted_iota(jnp.int32, one_hot_ref.shape, 0)
    rows = lax.rem(rows, table_rows)
    one_hot_ref[...] = jnp.where(rows == index_ref[...], 1.0, 0.0).astype(BF16)


def exact_parts(table):
    high = table.astype(BF16)
    rest = table - high.astype(F32)
    middle = rest.astype(BF16)
    low = (rest - middle.astype(F32)).astype(BF16)
    return jnp.concatenate([high, middle, low], axis=1)


def fetch_weight(slots, weight_hbm, weight_out, sems):
    rows = weight_out.shape[0] // slots
    out_cols = weight_out.shape[1]
    column = pl.multiple_of(lax.axis_index("head") * out_cols, out_cols)
    copies = []
    for slot in range(slots):
        start = pl.multiple_of(quarter_of(slot, slots) * rows, rows)
        copies.append(
            pltpu.make_async_copy(
                weight_hbm.at[pl.ds(start, rows), pl.ds(column, out_cols)],
                weight_out.at[pl.ds(slot * rows, rows), :],
                sems.at[slot],
            )
        )
        copies[-1].start()
    return copies


def local_levels(
    head_dim, first_head, query_ref, key_ref, value_ref, cos_ref, sin_ref, bucket_ref,
    weight_ref, query_out, combined_out
):
    tok_rows, width = query_out.shape
    stretch_len = tok_rows // STRETCHES_DEV
    groups = bucket_groups()
    shape = (stretch_len, stretch_len)
    causal = lax.broadcasted_iota(jnp.int32, shape, 0) >= lax.broadcasted_iota(jnp.int32, shape, 1)
    stride = weight_ref.shape[1] // bucket_ref.shape[0]
    spans = [
        slice(stretch * stretch_len, (stretch + 1) * stretch_len)
        for stretch in range(STRETCHES_DEV)
    ]
    plan = local_plan(STRETCHES_DEV)
    for spot in range(width // head_dim):
        head = first_head + spot
        cols = slice(head * head_dim, (head + 1) * head_dim)
        outs = slice(spot * head_dim, (spot + 1) * head_dim)
        weights = weight_ref[:, head * stride : head * stride + len(plan)]
        turned = [
            rotated(query_ref[rows, cols], cos_ref[rows, :], sin_ref[rows, :]) for rows in spans
        ]
        scores = [dot_nt(turned[i], key_ref[rows, cols]) for i, rows in enumerate(spans)]
        reads = [
            [
                (bit, dot_nn(turned[i], bucket_ref[head, groups.index(members)]))
                for bit, members in plan[i]
            ]
            for i in range(STRETCHES_DEV)
        ]
        scores = [jnp.where(causal, block, 0.0).astype(BF16) for block in scores]
        totals = [dot_nn(scores[i], value_ref[rows, cols]) for i, rows in enumerate(spans)]
        for i, rows in enumerate(spans):
            totals[i] = weights[rows, 0:1] * totals[i]
            for bit, read in reads[i]:
                totals[i] = totals[i] + weights[rows, bit + 1 : bit + 2] * read
        for i, rows in enumerate(spans):
            query_out[rows, outs] = turned[i]
            combined_out[rows, outs] = totals[i]


def first_local_kernel(
    slots,
    head_dim,
    levels,
    index_ref,
    table_ref,
    out_weight_hbm,
    query_ref,
    key_ref,
    value_ref,
    cos_ref,
    sin_ref,
    bucket_ref,
    weight_out,
    out_weight_out,
    query_out,
    combined_out,
    one_hot_ref,
    sems,
):
    copies = fetch_weight(slots, out_weight_hbm, out_weight_out, sems)
    fill_one_hot(index_ref, one_hot_ref)
    quarter_heads = table_ref.shape[1] // slots
    table_rows = table_ref.shape[2]
    stride = weight_out.shape[1] // table_ref.shape[1]
    stretch_len = weight_out.shape[0] // STRETCHES_DEV
    level = lax.broadcasted_iota(jnp.int32, (levels, table_rows), 0)
    scale = jnp.zeros((levels, table_rows), F32)
    for index in range(levels):
        scale = jnp.where(level == index, level_scale(index, stretch_len), scale)
    tables = []
    for slot in range(slots):
        for spot in range(quarter_heads):
            head = quarter_of(slot, slots) * quarter_heads + spot
            tables.append(table_ref[:, pl.ds(head, 1), :].reshape(levels, table_rows) * scale)
            if stride > levels:
                tables.append(jnp.zeros((stride - levels, table_rows), F32))
    parts = exact_parts(jnp.concatenate(tables, axis=0))
    weight_out[...] = dot_nn(parts, one_hot_ref[...]).T
    local_levels(
        head_dim, 0, query_ref, key_ref, value_ref, cos_ref, sin_ref, bucket_ref,
        weight_out, query_out, combined_out
    )
    for copy in copies:
        copy.wait()


def second_local_kernel(
    slots,
    head_dim,
    out_weight_hbm,
    query_ref,
    key_ref,
    value_ref,
    cos_ref,
    sin_ref,
    bucket_ref,
    weight_ref,
    out_weight_out,
    query_out,
    combined_out,
    sems,
):
    copies = fetch_weight(slots, out_weight_hbm, out_weight_out, sems)
    local_levels(
        head_dim, bucket_ref.shape[0] // 2, query_ref, key_ref, value_ref, cos_ref,
        sin_ref, bucket_ref, weight_ref, query_out, combined_out
    )
    for copy in copies:
        copy.wait()


def low_kernel(slots, low_bits, *refs):
    parts = [ref[...].astype(F32) for ref in refs[:slots]]
    total_out, *low_outs = refs[slots:]
    quarter_heads = parts[0].shape[0]
    total_out[...] = sum(parts).astype(BF16)
    for by in range(slots):
        for bit in range(low_bits):
            members = [m ^ by for m in range(slots) if m >> bit == 1]
            rows = slice(bit * quarter_heads, (bit + 1) * quarter_heads)
            low_outs[by][rows] = sum(parts[m] for m in members).astype(BF16)


def high_kernel(first_bit, bit_counts, *refs):
    *back_refs, out_ref = refs
    shard_index = lax.axis_index("ctx")
    quarter_heads = back_refs[0].shape[0]
    spot = 0
    level = 0
    for bits in bit_counts:
        radix = 1 << bits
        back = [ref[...].astype(F32) for ref in back_refs[spot : spot + radix - 1]]
        spot += radix - 1
        digit = shard_index >> (first_bit + level) & (radix - 1)
        out_ref[level * quarter_heads : (level + 1) * quarter_heads] = back[0].astype(BF16)
        level += 1
        if bits == 2:
            both = jnp.where(digit == 2, back[0] + back[1], back[1] + back[2])
            out_ref[level * quarter_heads : (level + 1) * quarter_heads] = both.astype(BF16)
            level += 1


def cross_kernel(
    first_slot,
    slots,
    all_slots,
    head_dim,
    levels,
    low_levels,
    high_levels,
    combined_ref,
    query_ref,
    weight_ref,
    gain_ref,
    *refs,
):
    low_refs = refs[:slots]
    high_refs = refs[slots : 2 * slots]
    hidden_out = refs[2 * slots]
    quarter_heads = hidden_out.shape[1] // head_dim // slots
    stride = weight_ref.shape[1] // (all_slots * quarter_heads)
    shard_index = lax.axis_index("ctx")
    cross_levels = low_levels + high_levels
    present = [(shard_index >> bit & 1).astype(F32) for bit in range(cross_levels)]
    for slot in range(slots):
        for spot in range(quarter_heads):
            here = slot * quarter_heads + spot
            head = first_slot * quarter_heads + here
            cols = slice(here * head_dim, (here + 1) * head_dim)
            total = combined_ref[:, cols]
            queries = query_ref[:, cols]
            for level in range(cross_levels):
                if level < low_levels:
                    bucket = low_refs[slot][level * quarter_heads + spot]
                else:
                    bucket = high_refs[slot][(level - low_levels) * quarter_heads + spot]
                column = head * stride + levels - cross_levels + level
                weight = weight_ref[:, column : column + 1] * present[level]
                total = total + weight * dot_nn(queries, bucket)
            mean_square = jnp.mean(total * total, axis=-1, keepdims=True)
            source = quarter_of(first_slot + slot, all_slots) * quarter_heads + spot
            gain = gain_ref[pl.ds(source, 1), :]
            normed = total * lax.rsqrt(mean_square + NORM_EPS) * gain
            hidden_out[:, cols] = normed.astype(BF16)


def early_kernel(tile, own_first, own_second, other_first, own_weight, other_weight, out_ref):
    depth = own_first.shape[1]
    for start in range(0, out_ref.shape[1], tile):
        cols = slice(start, start + tile)
        out_ref[:, cols] = (
            dot_nn(own_first[...], own_weight[0:depth, cols])
            + dot_nn(own_second[...], own_weight[depth:, cols])
            + dot_nn(other_first[...], other_weight[0:depth, cols])
        )


def late_kernel(tile, other_second, other_weight, part_ref, out_hbm, out_ref, sems):
    depth = other_second.shape[1]
    copies = []
    for index, start in enumerate(range(0, out_ref.shape[1], tile)):
        cols = slice(start, start + tile)
        total = part_ref[:, cols] + dot_nn(other_second[...], other_weight[depth:, cols])
        out_ref[:, cols] = total.astype(BF16)
        copies.append(
            pltpu.make_async_copy(out_ref.at[:, cols], out_hbm.at[:, cols], sems.at[index])
        )
        copies[-1].start()
    for copy in copies:
        copy.wait()


def call(kernel, name, operands, in_spaces, out_shapes, out_spaces, scratch, limit, flops, size):
    return pl.pallas_call(
        kernel,
        in_specs=[pl.BlockSpec(memory_space=space) for space in in_spaces],
        out_specs=[pl.BlockSpec(memory_space=space) for space in out_spaces],
        out_shape=out_shapes,
        scratch_shapes=scratch,
        compiler_params=pltpu.CompilerParams(vmem_limit_bytes=limit),
        cost_estimate=pl.CostEstimate(
            flops=int(flops), bytes_accessed=int(size), transcendentals=0
        ),
        name=name,
    )(*operands)


def local(queries, key_vectors, values, level_table, weight_index, norm_gain, out_weight):
    tok_rows, model_width = queries.shape
    table_rows, heads_here, levels = level_table.shape
    head_dim = model_width // heads_here
    stretch_len = tok_rows // STRETCHES_DEV
    n_ctx = lax.axis_size("ctx")
    n_head = lax.axis_size("head")
    ctx_bits = n_ctx.bit_length() - 1
    group_count = len(bucket_groups())
    low_bits = min(2, ctx_bits)
    high_bits = ctx_bits - low_bits
    slots = 1 << low_bits
    quarter_heads = heads_here // slots
    chunk = slots // 2
    half_width = model_width // 2
    out_cols = out_weight.shape[1] // n_head
    ANY, VMEM = pl.ANY, pltpu.VMEM

    def swap_heads(block):
        return lax.ppermute(block, "head", [(i, i ^ 1) for i in range(n_head)])

    def swap_low(block, by):
        return lax.ppermute(block, "ctx", [(i, i ^ by) for i in range(n_ctx)])

    coarse = tok_rows // FINE
    angles = np.concatenate(
        angle_rows(np.arange(FINE), head_dim)
        + angle_rows(np.arange(coarse) * FINE, head_dim)
        + angle_rows(np.arange(n_ctx) * tok_rows, head_dim)
    )
    head_macs = tok_rows * head_dim * head_dim
    block_bytes = tok_rows * model_width * 2

    def share(count=quarter_heads):
        return VMEM((count, head_dim, head_dim), BF16)

    block = VMEM((tok_rows, model_width), BF16)
    angle_block = VMEM((tok_rows, head_dim), F32)
    moved, moved_values, keys, cosine, sine, local_states, *shares = call(
        functools.partial(state_kernel, slots, head_dim, n_ctx),
        "states",
        (angles, queries, key_vectors, values),
        [ANY] * 4,
        [
            block,
            block,
            block,
            angle_block,
            angle_block,
            VMEM((heads_here, group_count, head_dim, head_dim), BF16),
        ]
        + [share()] * slots,
        [VMEM] * (6 + slots),
        [block, VMEM(angles.shape, F32), pltpu.SemaphoreType.DMA((4, slots))],
        FETCH_LIMIT,
        4 * head_macs * heads_here,
        4 * block_bytes,
    )

    out_weight, shares = lax.optimization_barrier((out_weight, shares))
    parts = [shares[0]] + [swap_low(shares[by], by) for by in range(1, slots)]
    other_weight = swap_heads(out_weight)

    half = VMEM((tok_rows, half_width), BF16)
    half_wide = VMEM((tok_rows, half_width), F32)
    weight_block = VMEM((model_width, out_cols), BF16)
    stride = -(-levels // 8) * 8
    level_block = VMEM((tok_rows, heads_here * stride), F32)
    inputs = (moved, keys, moved_values, cosine, sine, local_states)
    level_weights, own_weight, first_queries, first_combined = call(
        functools.partial(first_local_kernel, slots, head_dim, levels),
        "local_levels_first",
        (weight_index.reshape(1, tok_rows), level_table.transpose(2, 1, 0), out_weight) + inputs,
        [VMEM, VMEM, ANY] + [VMEM] * len(inputs),
        [level_block, weight_block, half, half_wide],
        [VMEM] * 4,
        [VMEM((3 * table_rows, tok_rows), BF16), pltpu.SemaphoreType.DMA((slots,))],
        LOCAL_LIMIT,
        3 * head_macs * heads_here,
        2 * block_bytes,
    )
    parts, inputs, level_weights = lax.optimization_barrier((parts, inputs, level_weights))

    low_count = low_bits * quarter_heads
    high_count = high_bits * quarter_heads
    total, *low_payloads = call(
        functools.partial(low_kernel, slots, low_bits),
        "low_buckets",
        parts,
        [VMEM] * slots,
        [share()] + [share(low_count)] * slots,
        [VMEM] * (1 + slots),
        [],
        SMALL_LIMIT,
        0,
        block_bytes,
    )

    back, bit_counts = [], []
    running = total
    for low in range(low_bits, ctx_bits, 2):
        bits = min(2, ctx_bits - low)
        radix = 1 << bits
        mask = (radix - 1) << low

        def turned(index, by):
            return index & ~mask | (((index >> low) + by) & (radix - 1)) << low

        arrived = [
            lax.ppermute(running, "ctx", [(i, turned(i, by)) for i in range(n_ctx)])
            for by in range(1, radix)
        ]
        back += arrived
        bit_counts.append(bits)
        if low + bits < ctx_bits:
            running = sum(a.astype(F32) for a in [running] + arrived).astype(BF16)

    low_slots = [low_payloads[0]] + [swap_low(low_payloads[by], by) for by in range(1, slots)]
    (high,) = call(
        functools.partial(high_kernel, low_bits, tuple(bit_counts)),
        "high_buckets",
        back,
        [VMEM] * len(back),
        [share(high_count)],
        [VMEM],
        [],
        SMALL_LIMIT,
        0,
        block_bytes,
    )
    high_slots = [high] + [swap_low(high, by) for by in range(1, slots)]

    other_block, second_queries, second_combined = call(
        functools.partial(second_local_kernel, slots, head_dim),
        "local_levels_second",
        (other_weight,) + inputs + (level_weights,),
        [ANY] + [VMEM] * (len(inputs) + 1),
        [weight_block, half, half_wide],
        [VMEM] * 3,
        [pltpu.SemaphoreType.DMA((slots,))],
        LOCAL_LIMIT,
        3 * head_macs * heads_here,
        2 * block_bytes,
    )

    gain, second_combined = lax.optimization_barrier((norm_gain, second_combined))
    gain = gain.reshape(heads_here, head_dim)
    hidden = []
    for first, combined, rotated_queries in (
        (0, first_combined, first_queries),
        (chunk, second_combined, second_queries),
    ):
        operands = (
            combined,
            rotated_queries,
            level_weights,
            gain,
            *low_slots[first : first + chunk],
            *high_slots[first : first + chunk],
        )
        (piece,) = call(
            functools.partial(
                cross_kernel, first, chunk, slots, head_dim, levels, low_bits, high_bits
            ),
            "cross_levels",
            operands,
            [VMEM] * len(operands),
            [half],
            [VMEM],
            [],
            SMALL_LIMIT,
            ctx_bits * head_macs * heads_here,
            block_bytes,
        )
        hidden.append(piece)
    other_hidden = [swap_heads(piece) for piece in hidden]

    tile = min(256, out_cols)
    (part,) = call(
        functools.partial(early_kernel, tile),
        "early_projection",
        (hidden[0], hidden[1], other_hidden[0], own_weight, other_block),
        [VMEM] * 5,
        [VMEM((tok_rows, out_cols), F32)],
        [VMEM],
        [],
        SMALL_LIMIT,
        3 * tok_rows * model_width * out_cols,
        2 * block_bytes,
    )
    (mixed_out,) = call(
        functools.partial(late_kernel, tile),
        "late_projection",
        (other_hidden[1], other_block, part),
        [VMEM] * 3,
        [jax.ShapeDtypeStruct((tok_rows, out_cols), BF16)],
        [ANY],
        [VMEM((tok_rows, out_cols), BF16), pltpu.SemaphoreType.DMA((out_cols // tile,))],
        SMALL_LIMIT,
        tok_rows * model_width * out_cols,
        2 * block_bytes,
    )
    return mixed_out


def solution(mesh):
    return jax.shard_map(
        local,
        mesh=mesh,
        in_specs=(
            P("ctx", "head"),
            P("ctx", "head"),
            P("ctx", "head"),
            P(None, "head", None),
            P("ctx"),
            P("head"),
            P("head", None),
        ),
        out_specs=P("ctx", "head"),
        check_vma=False,
    )
```

```python
import functools
import math

import jax
import jax.numpy as jnp
import numpy as np
from jax import lax
from jax.experimental import pallas as pl
from jax.experimental.pallas import tpu as pltpu
from jax.sharding import PartitionSpec as P

STRETCHES_DEV = 4
ROPE_BASE = 500000.0
NORM_EPS = 1e-06
FETCH_LIMIT = 59 << 20
LOCAL_LIMIT = 42 << 20
SMALL_LIMIT = 20 << 20
FINE = 16

F32 = jnp.float32
BF16 = jnp.bfloat16


def angle_rows(positions, head_dim):
    half_dim = head_dim // 2
    frequency = np.exp(np.arange(half_dim) * (-2.0 * math.log(ROPE_BASE) / head_dim))
    angles = np.asarray(positions, np.float64)[:, None] * frequency[None, :]
    cosine, sine = np.cos(angles), np.sin(angles)
    return [
        np.concatenate([cosine, cosine], axis=1).astype(np.float32),
        np.concatenate([-sine, sine], axis=1).astype(np.float32),
    ]


def level_scale(level_index, stretch_len):
    if level_index == 0:
        return stretch_len ** (-0.5)
    return (2 ** (level_index - 1) * stretch_len) ** (-0.5)


def quarter_of(slot, slots):
    return slot ^ (lax.axis_index("ctx") & (slots - 1))


def turn_sum(cos_a, sin_a, cos_b, sin_b):
    return cos_a * cos_b - sin_a * sin_b, sin_a * cos_b + cos_a * sin_b


def fill_angles(angle_ref, shard_index, n_ctx, cos_ref, sin_ref):
    coarse = cos_ref.shape[0] // FINE
    fine_cos, fine_sin = angle_ref[0:FINE, :], angle_ref[FINE : 2 * FINE, :]
    first = 2 * FINE
    coarse_cos = angle_ref[first : first + coarse, :]
    coarse_sin = angle_ref[first + coarse : first + 2 * coarse, :]
    first += 2 * coarse
    base_cos = angle_ref[pl.ds(first + shard_index, 1), :]
    base_sin = angle_ref[pl.ds(first + n_ctx + shard_index, 1), :]
    coarse_cos, coarse_sin = turn_sum(coarse_cos, coarse_sin, base_cos, base_sin)
    for index in range(coarse):
        rows = slice(index * FINE, (index + 1) * FINE)
        cos_ref[rows, :], sin_ref[rows, :] = turn_sum(
            coarse_cos[index : index + 1, :], coarse_sin[index : index + 1, :], fine_cos, fine_sin
        )


def rotated(vectors, cosine, sine):
    wide = vectors.astype(F32)
    half = wide.shape[-1] // 2
    return (wide * cosine + pltpu.roll(wide, half, 1) * sine).astype(BF16)


def dot_tn(a, b):
    return lax.dot_general(a, b, (((0,), (0,)), ((), ())), preferred_element_type=F32)


def dot_nt(a, b):
    return lax.dot_general(a, b, (((1,), (1,)), ((), ())), preferred_element_type=F32)


def dot_nn(a, b):
    return jnp.dot(a, b, preferred_element_type=F32)


def local_plan(stretches):
    plan = []
    for stretch in range(stretches):
        row = []
        for bit in range(stretches.bit_length() - 1):
            if stretch >> bit & 1:
                end = stretch >> bit << bit
                row.append((bit, tuple(range(end - (1 << bit), end))))
        plan.append(row)
    return plan


def state_kernel(
    slots,
    head_dim,
    n_ctx,
    angle_hbm,
    query_hbm,
    key_hbm,
    value_hbm,
    query_out,
    value_out,
    key_out,
    cos_out,
    sin_out,
    bucket_out,
    *refs,
):
    total_outs = refs[:slots]
    key_raw, angle_ref, sems = refs[slots:]
    tok_rows, model_width = key_raw.shape
    width = model_width // slots

    def fetch(source, target, slot, sem):
        start = pl.multiple_of(quarter_of(slot, slots) * width, width)
        return pltpu.make_async_copy(
            source.at[:, pl.ds(start, width)], target.at[:, pl.ds(slot * width, width)], sem
        )

    angles_in = pltpu.make_async_copy(angle_hbm, angle_ref, sems.at[3, 0])
    angles_in.start()
    order = list(range(slots - 1, -1, -1))
    copies = {}
    for kind, (source, target) in enumerate(
        ((key_hbm, key_raw), (value_hbm, value_out), (query_hbm, query_out))
    ):
        for slot in order:
            copies[kind, slot] = fetch(source, target, slot, sems.at[kind, slot])
    for slot in order:
        copies[0, slot].start()
        copies[1, slot].start()
    for slot in range(slots):
        copies[2, slot].start()
    angles_in.wait()
    fill_angles(angle_ref, lax.axis_index("ctx"), n_ctx, cos_out, sin_out)

    stretch_len = tok_rows // STRETCHES_DEV
    groups = bucket_groups()
    quarter_heads = width // head_dim
    for slot in order:
        copies[0, slot].wait()
        copies[1, slot].wait()
        heads = range(slot * quarter_heads, (slot + 1) * quarter_heads)
        turned, states = {}, {}
        for head in heads:
            cols = slice(head * head_dim, (head + 1) * head_dim)
            for stretch in range(STRETCHES_DEV):
                rows = slice(stretch * stretch_len, (stretch + 1) * stretch_len)
                block = rotated(key_raw[rows, cols], cos_out[rows, :], sin_out[rows, :])
                turned[head, stretch] = block
                states[head, stretch] = dot_tn(block, value_out[rows, cols])
        for head in heads:
            cols = slice(head * head_dim, (head + 1) * head_dim)
            for stretch in range(STRETCHES_DEV):
                rows = slice(stretch * stretch_len, (stretch + 1) * stretch_len)
                key_out[rows, cols] = turned[head, stretch]
            sums = {}
            for group, members in enumerate(groups):
                sums[members] = sum(states[head, m] for m in members)
                bucket_out[head, group] = sums[members].astype(BF16)
            total = sum(states[head, m] for m in range(STRETCHES_DEV))
            total_outs[slot][head - heads[0]] = total.astype(BF16)
    for slot in range(slots):
        copies[2, slot].wait()


def bucket_groups():
    groups = []
    for row in local_plan(STRETCHES_DEV):
        for _, members in row:
            if members not in groups:
                groups.append(members)
    return groups


def fill_one_hot(index_ref, one_hot_ref):
    table_rows = one_hot_ref.shape[0] // 3
    rows = lax.broadcasted_iota(jnp.int32, one_hot_ref.shape, 0)
    rows = lax.rem(rows, table_rows)
    one_hot_ref[...] = jnp.where(rows == index_ref[...], 1.0, 0.0).astype(BF16)


def exact_parts(table):
    high = table.astype(BF16)
    rest = table - high.astype(F32)
    middle = rest.astype(BF16)
    low = (rest - middle.astype(F32)).astype(BF16)
    return jnp.concatenate([high, middle, low], axis=1)


def fetch_weight(slots, head_index, weight_hbm, weight_out, sems):
    rows = weight_out.shape[0] // slots
    out_cols = weight_out.shape[1]
    column = pl.multiple_of(head_index * out_cols, out_cols)
    copies = []
    for slot in range(slots):
        start = pl.multiple_of(quarter_of(slot, slots) * rows, rows)
        copies.append(
            pltpu.make_async_copy(
                weight_hbm.at[pl.ds(start, rows), pl.ds(column, out_cols)],
                weight_out.at[pl.ds(slot * rows, rows), :],
                sems.at[slot],
            )
        )
        copies[-1].start()
    return copies


def local_levels(
    head_dim, first_head, query_ref, key_ref, value_ref, cos_ref, sin_ref, bucket_ref,
    weight_ref, query_out, combined_out, low_refs=()
):
    tok_rows, width = query_out.shape
    stretch_len = tok_rows // STRETCHES_DEV
    groups = bucket_groups()
    shape = (stretch_len, stretch_len)
    causal = lax.broadcasted_iota(jnp.int32, shape, 0) >= lax.broadcasted_iota(jnp.int32, shape, 1)
    stride = weight_ref.shape[1] // bucket_ref.shape[0]
    spans = [
        slice(stretch * stretch_len, (stretch + 1) * stretch_len)
        for stretch in range(STRETCHES_DEV)
    ]
    plan = local_plan(STRETCHES_DEV)
    for spot in range(width // head_dim):
        head = first_head + spot
        cols = slice(head * head_dim, (head + 1) * head_dim)
        outs = slice(spot * head_dim, (spot + 1) * head_dim)
        weights = weight_ref[:, head * stride : head * stride + len(plan)]
        turned = [
            rotated(query_ref[rows, cols], cos_ref[rows, :], sin_ref[rows, :]) for rows in spans
        ]
        scores = [dot_nt(turned[i], key_ref[rows, cols]) for i, rows in enumerate(spans)]
        reads = [
            [
                (bit, dot_nn(turned[i], bucket_ref[head, groups.index(members)]))
                for bit, members in plan[i]
            ]
            for i in range(STRETCHES_DEV)
        ]
        scores = [jnp.where(causal, block, 0.0).astype(BF16) for block in scores]
        totals = [dot_nn(scores[i], value_ref[rows, cols]) for i, rows in enumerate(spans)]
        for i, rows in enumerate(spans):
            totals[i] = weights[rows, 0:1] * totals[i]
            for bit, read in reads[i]:
                totals[i] = totals[i] + weights[rows, bit + 1 : bit + 2] * read
        if low_refs:
            added = low_levels(
                jnp.concatenate(turned, axis=0), head, weight_ref, bucket_ref.shape[0], low_refs
            )
            totals = [totals[i] + added[rows] for i, rows in enumerate(spans)]
        for i, rows in enumerate(spans):
            query_out[rows, outs] = turned[i]
            combined_out[rows, outs] = totals[i]


def first_local_kernel(
    slots,
    head_dim,
    levels,
    index_ref,
    table_ref,
    out_weight_hbm,
    query_ref,
    key_ref,
    value_ref,
    cos_ref,
    sin_ref,
    bucket_ref,
    weight_out,
    own_weight_out,
    sent_weight_out,
    query_out,
    combined_out,
    one_hot_ref,
    sems,
):
    head_index = lax.axis_index("head")
    copies = fetch_weight(slots, head_index, out_weight_hbm, own_weight_out, sems.at[0])
    copies += fetch_weight(slots, head_index ^ 1, out_weight_hbm, sent_weight_out, sems.at[1])
    fill_one_hot(index_ref, one_hot_ref)
    quarter_heads = table_ref.shape[1] // slots
    table_rows = table_ref.shape[2]
    stride = weight_out.shape[1] // table_ref.shape[1]
    stretch_len = weight_out.shape[0] // STRETCHES_DEV
    level = lax.broadcasted_iota(jnp.int32, (levels, table_rows), 0)
    scale = jnp.zeros((levels, table_rows), F32)
    for index in range(levels):
        scale = jnp.where(level == index, level_scale(index, stretch_len), scale)
    tables = []
    for slot in range(slots):
        for spot in range(quarter_heads):
            head = quarter_of(slot, slots) * quarter_heads + spot
            tables.append(table_ref[:, pl.ds(head, 1), :].reshape(levels, table_rows) * scale)
            if stride > levels:
                tables.append(jnp.zeros((stride - levels, table_rows), F32))
    parts = exact_parts(jnp.concatenate(tables, axis=0))
    weight_out[...] = dot_nn(parts, one_hot_ref[...]).T
    local_levels(
        head_dim, 0, query_ref, key_ref, value_ref, cos_ref, sin_ref, bucket_ref,
        weight_out, query_out, combined_out
    )
    for copy in copies:
        copy.wait()


def low_levels(queries, head, weight_ref, heads, low_refs):
    slots = len(low_refs)
    quarter_heads = heads // slots
    stride = weight_ref.shape[1] // heads
    low_bits = low_refs[0].shape[0] // quarter_heads
    first = len(local_plan(STRETCHES_DEV)[-1]) + 1
    shard_index = lax.axis_index("ctx")
    total = None
    for bit in range(low_bits):
        bucket = low_refs[head // quarter_heads][bit * quarter_heads + head % quarter_heads]
        column = head * stride + first + bit
        present = (shard_index >> bit & 1).astype(F32)
        part = weight_ref[:, column : column + 1] * present * dot_nn(queries, bucket)
        total = part if total is None else total + part
    return total


def second_local_kernel(
    head_dim,
    query_ref,
    key_ref,
    value_ref,
    cos_ref,
    sin_ref,
    bucket_ref,
    weight_ref,
    first_query_ref,
    first_combined_ref,
    *refs,
):
    *low_refs, first_combined_out, query_out, combined_out = refs
    heads = bucket_ref.shape[0]
    for head in range(heads // 2):
        cols = slice(head * head_dim, (head + 1) * head_dim)
        first_combined_out[:, cols] = first_combined_ref[:, cols] + low_levels(
            first_query_ref[:, cols], head, weight_ref, heads, low_refs
        )
    local_levels(
        head_dim, heads // 2, query_ref, key_ref, value_ref, cos_ref, sin_ref, bucket_ref,
        weight_ref, query_out, combined_out, low_refs
    )


def low_kernel(slots, low_bits, *refs):
    parts = [ref[...].astype(F32) for ref in refs[:slots]]
    total_out, *low_outs = refs[slots:]
    quarter_heads = parts[0].shape[0]
    total_out[...] = sum(parts).astype(BF16)
    for by in range(slots):
        for bit in range(low_bits):
            members = [m ^ by for m in range(slots) if m >> bit == 1]
            rows = slice(bit * quarter_heads, (bit + 1) * quarter_heads)
            low_outs[by][rows] = sum(parts[m] for m in members).astype(BF16)


def high_kernel(first_bit, bit_counts, *refs):
    *back_refs, out_ref = refs
    shard_index = lax.axis_index("ctx")
    quarter_heads = back_refs[0].shape[0]
    spot = 0
    level = 0
    for bits in bit_counts:
        radix = 1 << bits
        back = [ref[...].astype(F32) for ref in back_refs[spot : spot + radix - 1]]
        spot += radix - 1
        digit = shard_index >> (first_bit + level) & (radix - 1)
        out_ref[level * quarter_heads : (level + 1) * quarter_heads] = back[0].astype(BF16)
        level += 1
        if bits == 2:
            both = jnp.where(digit == 2, back[0] + back[1], back[1] + back[2])
            out_ref[level * quarter_heads : (level + 1) * quarter_heads] = both.astype(BF16)
            level += 1


def cross_kernel(
    first_slot,
    slots,
    all_slots,
    head_dim,
    levels,
    high_levels,
    combined_ref,
    query_ref,
    weight_ref,
    gain_ref,
    *refs,
):
    *high_refs, hidden_out = refs
    quarter_heads = hidden_out.shape[1] // head_dim // slots
    stride = weight_ref.shape[1] // (all_slots * quarter_heads)
    shard_index = lax.axis_index("ctx")
    first_bit = all_slots.bit_length() - 1
    present = [
        (shard_index >> (first_bit + bit) & 1).astype(F32) for bit in range(high_levels)
    ]
    for slot in range(slots):
        for spot in range(quarter_heads):
            here = slot * quarter_heads + spot
            head = first_slot * quarter_heads + here
            cols = slice(here * head_dim, (here + 1) * head_dim)
            total = combined_ref[:, cols]
            queries = query_ref[:, cols]
            for level in range(high_levels):
                bucket = high_refs[slot][level * quarter_heads + spot]
                column = head * stride + levels - high_levels + level
                weight = weight_ref[:, column : column + 1] * present[level]
                total = total + weight * dot_nn(queries, bucket)
            mean_square = jnp.mean(total * total, axis=-1, keepdims=True)
            source = quarter_of(first_slot + slot, all_slots) * quarter_heads + spot
            gain = gain_ref[pl.ds(source, 1), :]
            normed = total * lax.rsqrt(mean_square + NORM_EPS) * gain
            hidden_out[:, cols] = normed.astype(BF16)


def early_kernel(tile, own_first, own_second, other_first, own_weight, other_weight, out_ref):
    depth = own_first.shape[1]
    for start in range(0, out_ref.shape[1], tile):
        cols = slice(start, start + tile)
        out_ref[:, cols] = (
            dot_nn(own_first[...], own_weight[0:depth, cols])
            + dot_nn(own_second[...], own_weight[depth:, cols])
            + dot_nn(other_first[...], other_weight[0:depth, cols])
        )


def late_kernel(tile, other_second, other_weight, part_ref, out_hbm, out_ref, sems):
    depth = other_second.shape[1]
    copies = []
    for index, start in enumerate(range(0, out_ref.shape[1], tile)):
        cols = slice(start, start + tile)
        total = part_ref[:, cols] + dot_nn(other_second[...], other_weight[depth:, cols])
        out_ref[:, cols] = total.astype(BF16)
        copies.append(
            pltpu.make_async_copy(out_ref.at[:, cols], out_hbm.at[:, cols], sems.at[index])
        )
        copies[-1].start()
    for copy in copies:
        copy.wait()


def call(kernel, name, operands, in_spaces, out_shapes, out_spaces, scratch, limit, flops, size):
    return pl.pallas_call(
        kernel,
        in_specs=[pl.BlockSpec(memory_space=space) for space in in_spaces],
        out_specs=[pl.BlockSpec(memory_space=space) for space in out_spaces],
        out_shape=out_shapes,
        scratch_shapes=scratch,
        compiler_params=pltpu.CompilerParams(vmem_limit_bytes=limit),
        cost_estimate=pl.CostEstimate(
            flops=int(flops), bytes_accessed=int(size), transcendentals=0
        ),
        name=name,
    )(*operands)


def local(queries, key_vectors, values, level_table, weight_index, norm_gain, out_weight):
    tok_rows, model_width = queries.shape
    table_rows, heads_here, levels = level_table.shape
    head_dim = model_width // heads_here
    stretch_len = tok_rows // STRETCHES_DEV
    n_ctx = lax.axis_size("ctx")
    n_head = lax.axis_size("head")
    ctx_bits = n_ctx.bit_length() - 1
    group_count = len(bucket_groups())
    low_bits = min(2, ctx_bits)
    high_bits = ctx_bits - low_bits
    slots = 1 << low_bits
    quarter_heads = heads_here // slots
    chunk = slots // 2
    half_width = model_width // 2
    out_cols = out_weight.shape[1] // n_head
    ANY, VMEM = pl.ANY, pltpu.VMEM

    def swap_heads(block):
        return lax.ppermute(block, "head", [(i, i ^ 1) for i in range(n_head)])

    def swap_low(block, by):
        return lax.ppermute(block, "ctx", [(i, i ^ by) for i in range(n_ctx)])

    coarse = tok_rows // FINE
    angles = np.concatenate(
        angle_rows(np.arange(FINE), head_dim)
        + angle_rows(np.arange(coarse) * FINE, head_dim)
        + angle_rows(np.arange(n_ctx) * tok_rows, head_dim)
    )
    head_macs = tok_rows * head_dim * head_dim
    block_bytes = tok_rows * model_width * 2

    def share(count=quarter_heads):
        return VMEM((count, head_dim, head_dim), BF16)

    block = VMEM((tok_rows, model_width), BF16)
    angle_block = VMEM((tok_rows, head_dim), F32)
    moved, moved_values, keys, cosine, sine, local_states, *shares = call(
        functools.partial(state_kernel, slots, head_dim, n_ctx),
        "states",
        (angles, queries, key_vectors, values),
        [ANY] * 4,
        [
            block,
            block,
            block,
            angle_block,
            angle_block,
            VMEM((heads_here, group_count, head_dim, head_dim), BF16),
        ]
        + [share()] * slots,
        [VMEM] * (6 + slots),
        [block, VMEM(angles.shape, F32), pltpu.SemaphoreType.DMA((4, slots))],
        FETCH_LIMIT,
        4 * head_macs * heads_here,
        4 * block_bytes,
    )

    parts = [shares[0]] + [swap_low(shares[by], by) for by in range(1, slots)]
    half = VMEM((tok_rows, half_width), BF16)
    half_wide = VMEM((tok_rows, half_width), F32)
    weight_block = VMEM((model_width, out_cols), BF16)
    stride = -(-levels // 8) * 8
    level_block = VMEM((tok_rows, heads_here * stride), F32)
    inputs = (moved, keys, moved_values, cosine, sine, local_states)
    level_weights, own_weight, sent_weight, first_queries, first_combined = call(
        functools.partial(first_local_kernel, slots, head_dim, levels),
        "local_levels_first",
        (weight_index.reshape(1, tok_rows), level_table.transpose(2, 1, 0), out_weight) + inputs,
        [VMEM, VMEM, ANY] + [VMEM] * len(inputs),
        [level_block, weight_block, weight_block, half, half_wide],
        [VMEM] * 5,
        [VMEM((3 * table_rows, tok_rows), BF16), pltpu.SemaphoreType.DMA((2, slots))],
        LOCAL_LIMIT,
        3 * head_macs * heads_here,
        2 * block_bytes,
    )
    parts, inputs, level_weights, sent_weight = lax.optimization_barrier(
        (parts, inputs, level_weights, sent_weight)
    )
    other_block = swap_heads(sent_weight)

    low_count = low_bits * quarter_heads
    high_count = high_bits * quarter_heads
    total, *low_payloads = call(
        functools.partial(low_kernel, slots, low_bits),
        "low_buckets",
        parts,
        [VMEM] * slots,
        [share()] + [share(low_count)] * slots,
        [VMEM] * (1 + slots),
        [],
        SMALL_LIMIT,
        0,
        block_bytes,
    )

    back, bit_counts = [], []
    running = total
    for low in range(low_bits, ctx_bits, 2):
        bits = min(2, ctx_bits - low)
        radix = 1 << bits
        mask = (radix - 1) << low

        def turned(index, by):
            return index & ~mask | (((index >> low) + by) & (radix - 1)) << low

        arrived = [
            lax.ppermute(running, "ctx", [(i, turned(i, by)) for i in range(n_ctx)])
            for by in range(1, radix)
        ]
        back += arrived
        bit_counts.append(bits)
        if low + bits < ctx_bits:
            running = sum(a.astype(F32) for a in [running] + arrived).astype(BF16)

    low_slots = [low_payloads[0]] + [swap_low(low_payloads[by], by) for by in range(1, slots)]
    (high,) = call(
        functools.partial(high_kernel, low_bits, tuple(bit_counts)),
        "high_buckets",
        back,
        [VMEM] * len(back),
        [share(high_count)],
        [VMEM],
        [],
        SMALL_LIMIT,
        0,
        block_bytes,
    )
    high_slots = [high] + [swap_low(high, by) for by in range(1, slots)]

    operands = inputs + (level_weights, first_queries, first_combined, *low_slots)
    first_combined, second_queries, second_combined = call(
        functools.partial(second_local_kernel, head_dim),
        "local_levels_second",
        operands,
        [VMEM] * len(operands),
        [half_wide, half, half_wide],
        [VMEM] * 3,
        [],
        SMALL_LIMIT,
        5 * head_macs * heads_here,
        2 * block_bytes,
    )

    gain, second_combined = lax.optimization_barrier((norm_gain, second_combined))
    gain = gain.reshape(heads_here, head_dim)
    hidden = []
    for first, combined, rotated_queries in (
        (0, first_combined, first_queries),
        (chunk, second_combined, second_queries),
    ):
        operands = (
            combined,
            rotated_queries,
            level_weights,
            gain,
            *high_slots[first : first + chunk],
        )
        (piece,) = call(
            functools.partial(
                cross_kernel, first, chunk, slots, head_dim, levels, high_bits
            ),
            "cross_levels",
            operands,
            [VMEM] * len(operands),
            [half],
            [VMEM],
            [],
            SMALL_LIMIT,
            ctx_bits * head_macs * heads_here,
            block_bytes,
        )
        hidden.append(piece)
    other_hidden = [swap_heads(piece) for piece in hidden]

    tile = min(256, out_cols)
    (part,) = call(
        functools.partial(early_kernel, tile),
        "early_projection",
        (hidden[0], hidden[1], other_hidden[0], own_weight, other_block),
        [VMEM] * 5,
        [VMEM((tok_rows, out_cols), F32)],
        [VMEM],
        [],
        SMALL_LIMIT,
        3 * tok_rows * model_width * out_cols,
        2 * block_bytes,
    )
    (mixed_out,) = call(
        functools.partial(late_kernel, tile),
        "late_projection",
        (other_hidden[1], other_block, part),
        [VMEM] * 3,
        [jax.ShapeDtypeStruct((tok_rows, out_cols), BF16)],
        [ANY],
        [VMEM((tok_rows, out_cols), BF16), pltpu.SemaphoreType.DMA((out_cols // tile,))],
        SMALL_LIMIT,
        tok_rows * model_width * out_cols,
        2 * block_bytes,
    )
    return mixed_out


def solution(mesh):
    return jax.shard_map(
        local,
        mesh=mesh,
        in_specs=(
            P("ctx", "head"),
            P("ctx", "head"),
            P("ctx", "head"),
            P(None, "head", None),
            P("ctx"),
            P("head"),
            P("head", None),
        ),
        out_specs=P("ctx", "head"),
        check_vma=False,
    )
```

```python
import functools
import math

import jax
import jax.numpy as jnp
import numpy as np
from jax import lax
from jax.experimental import pallas as pl
from jax.experimental.pallas import tpu as pltpu
from jax.sharding import PartitionSpec as P

STRETCHES_DEV = 4
ROPE_BASE = 500000.0
NORM_EPS = 1e-06
FETCH_LIMIT = 59 << 20
LOCAL_LIMIT = 42 << 20
SMALL_LIMIT = 20 << 20
FINE = 16

F32 = jnp.float32
BF16 = jnp.bfloat16


def angle_rows(positions, head_dim):
    half_dim = head_dim // 2
    frequency = np.exp(np.arange(half_dim) * (-2.0 * math.log(ROPE_BASE) / head_dim))
    angles = np.asarray(positions, np.float64)[:, None] * frequency[None, :]
    cosine, sine = np.cos(angles), np.sin(angles)
    return [
        np.concatenate([cosine, cosine], axis=1).astype(np.float32),
        np.concatenate([-sine, sine], axis=1).astype(np.float32),
    ]


def level_scale(level_index, stretch_len):
    if level_index == 0:
        return stretch_len ** (-0.5)
    return (2 ** (level_index - 1) * stretch_len) ** (-0.5)


def quarter_of(slot, slots):
    return slot ^ (lax.axis_index("ctx") & (slots - 1))


def turn_sum(cos_a, sin_a, cos_b, sin_b):
    return cos_a * cos_b - sin_a * sin_b, sin_a * cos_b + cos_a * sin_b


def fill_angles(angle_ref, shard_index, n_ctx, cos_ref, sin_ref):
    coarse = cos_ref.shape[0] // FINE
    fine_cos, fine_sin = angle_ref[0:FINE, :], angle_ref[FINE : 2 * FINE, :]
    first = 2 * FINE
    coarse_cos = angle_ref[first : first + coarse, :]
    coarse_sin = angle_ref[first + coarse : first + 2 * coarse, :]
    first += 2 * coarse
    base_cos = angle_ref[pl.ds(first + shard_index, 1), :]
    base_sin = angle_ref[pl.ds(first + n_ctx + shard_index, 1), :]
    coarse_cos, coarse_sin = turn_sum(coarse_cos, coarse_sin, base_cos, base_sin)
    for index in range(coarse):
        rows = slice(index * FINE, (index + 1) * FINE)
        cos_ref[rows, :], sin_ref[rows, :] = turn_sum(
            coarse_cos[index : index + 1, :], coarse_sin[index : index + 1, :], fine_cos, fine_sin
        )


def rotated(vectors, cosine, sine):
    wide = vectors.astype(F32)
    half = wide.shape[-1] // 2
    return (wide * cosine + pltpu.roll(wide, half, 1) * sine).astype(BF16)


def dot_tn(a, b):
    return lax.dot_general(a, b, (((0,), (0,)), ((), ())), preferred_element_type=F32)


def dot_nt(a, b):
    return lax.dot_general(a, b, (((1,), (1,)), ((), ())), preferred_element_type=F32)


def dot_nn(a, b):
    return jnp.dot(a, b, preferred_element_type=F32)


def local_plan(stretches):
    plan = []
    for stretch in range(stretches):
        row = []
        for bit in range(stretches.bit_length() - 1):
            if stretch >> bit & 1:
                end = stretch >> bit << bit
                row.append((bit, tuple(range(end - (1 << bit), end))))
        plan.append(row)
    return plan


def head_columns(head, slots, heads, head_dim):
    slot, spot = divmod(head, heads // slots)
    source = quarter_of(slot, slots) * (heads // slots) + spot
    return pl.ds(pl.multiple_of(source * head_dim, head_dim), head_dim)


def state_kernel(
    slots,
    head_dim,
    n_ctx,
    angle_hbm,
    query_hbm,
    key_hbm,
    value_hbm,
    query_out,
    value_out,
    key_out,
    cos_out,
    sin_out,
    bucket_out,
    *refs,
):
    total_outs = refs[:slots]
    key_raw, angle_ref, sems = refs[slots:]
    tok_rows, model_width = key_raw.shape
    stretch_len = tok_rows // STRETCHES_DEV
    heads = range(model_width // head_dim)
    groups = bucket_groups()
    spans = [slice(i * stretch_len, (i + 1) * stretch_len) for i in range(STRETCHES_DEV)]

    angles_in = pltpu.make_async_copy(angle_hbm, angle_ref, sems.at[3, 0])
    angles_in.start()
    copies = [
        [
            pltpu.make_async_copy(source.at[rows, :], target.at[rows, :], sems.at[kind, index])
            for index, rows in enumerate(spans)
        ]
        for kind, (source, target) in enumerate(
            ((key_hbm, key_raw), (value_hbm, value_out), (query_hbm, query_out))
        )
    ]
    for index in range(STRETCHES_DEV):
        copies[0][index].start()
        copies[1][index].start()
    for copy in copies[2]:
        copy.start()
    angles_in.wait()
    fill_angles(angle_ref, lax.axis_index("ctx"), n_ctx, cos_out, sin_out)

    quarter_heads = len(heads) // slots
    states = {}
    for index, rows in enumerate(spans):
        copies[0][index].wait()
        copies[1][index].wait()
        blocks = []
        for head in heads:
            source = head_columns(head, slots, len(heads), head_dim)
            block = rotated(key_raw[rows, source], cos_out[rows, :], sin_out[rows, :])
            blocks.append(block)
            states[head, index] = dot_tn(block, value_out[rows, source])
        for head in heads:
            key_out[rows, head * head_dim : (head + 1) * head_dim] = blocks[head]
    for head in heads:
        for group, members in enumerate(groups):
            bucket_out[head, group] = sum(states[head, m] for m in members).astype(BF16)
        total = sum(states[head, m] for m in range(STRETCHES_DEV))
        total_outs[head // quarter_heads][head % quarter_heads] = total.astype(BF16)
    for copy in copies[2]:
        copy.wait()


def bucket_groups():
    groups = []
    for row in local_plan(STRETCHES_DEV):
        for _, members in row:
            if members not in groups:
                groups.append(members)
    return groups


def fill_one_hot(index_ref, one_hot_ref):
    table_rows = one_hot_ref.shape[0] // 3
    rows = lax.broadcasted_iota(jnp.int32, one_hot_ref.shape, 0)
    rows = lax.rem(rows, table_rows)
    one_hot_ref[...] = jnp.where(rows == index_ref[...], 1.0, 0.0).astype(BF16)


def exact_parts(table):
    high = table.astype(BF16)
    rest = table - high.astype(F32)
    middle = rest.astype(BF16)
    low = (rest - middle.astype(F32)).astype(BF16)
    return jnp.concatenate([high, middle, low], axis=1)


def fetch_weight(slots, head_index, weight_hbm, weight_out, sems):
    rows = weight_out.shape[0] // slots
    out_cols = weight_out.shape[1]
    column = pl.multiple_of(head_index * out_cols, out_cols)
    copies = []
    for slot in range(slots):
        start = pl.multiple_of(quarter_of(slot, slots) * rows, rows)
        copies.append(
            pltpu.make_async_copy(
                weight_hbm.at[pl.ds(start, rows), pl.ds(column, out_cols)],
                weight_out.at[pl.ds(slot * rows, rows), :],
                sems.at[slot],
            )
        )
        copies[-1].start()
    return copies


def local_levels(
    slots, head_dim, first_head, query_ref, key_ref, value_ref, cos_ref, sin_ref, bucket_ref,
    weight_ref, query_out, combined_out, low_refs=()
):
    tok_rows, width = query_out.shape
    stretch_len = tok_rows // STRETCHES_DEV
    groups = bucket_groups()
    shape = (stretch_len, stretch_len)
    causal = lax.broadcasted_iota(jnp.int32, shape, 0) >= lax.broadcasted_iota(jnp.int32, shape, 1)
    stride = weight_ref.shape[1] // bucket_ref.shape[0]
    spans = [
        slice(stretch * stretch_len, (stretch + 1) * stretch_len)
        for stretch in range(STRETCHES_DEV)
    ]
    plan = local_plan(STRETCHES_DEV)
    for spot in range(width // head_dim):
        head = first_head + spot
        cols = slice(head * head_dim, (head + 1) * head_dim)
        outs = slice(spot * head_dim, (spot + 1) * head_dim)
        source = head_columns(head, slots, bucket_ref.shape[0], head_dim)
        weights = weight_ref[:, head * stride : head * stride + len(plan)]
        turned = [
            rotated(query_ref[rows, source], cos_ref[rows, :], sin_ref[rows, :]) for rows in spans
        ]
        scores = [dot_nt(turned[i], key_ref[rows, cols]) for i, rows in enumerate(spans)]
        reads = [
            [
                (bit, dot_nn(turned[i], bucket_ref[head, groups.index(members)]))
                for bit, members in plan[i]
            ]
            for i in range(STRETCHES_DEV)
        ]
        scores = [jnp.where(causal, block, 0.0).astype(BF16) for block in scores]
        totals = [dot_nn(scores[i], value_ref[rows, source]) for i, rows in enumerate(spans)]
        for i, rows in enumerate(spans):
            totals[i] = weights[rows, 0:1] * totals[i]
            for bit, read in reads[i]:
                totals[i] = totals[i] + weights[rows, bit + 1 : bit + 2] * read
        if low_refs:
            added = low_levels(
                jnp.concatenate(turned, axis=0), head, weight_ref, bucket_ref.shape[0], low_refs
            )
            totals = [totals[i] + added[rows] for i, rows in enumerate(spans)]
        for i, rows in enumerate(spans):
            query_out[rows, outs] = turned[i]
            combined_out[rows, outs] = totals[i]


def first_local_kernel(
    slots,
    head_dim,
    levels,
    index_ref,
    table_ref,
    out_weight_hbm,
    query_ref,
    key_ref,
    value_ref,
    cos_ref,
    sin_ref,
    bucket_ref,
    weight_out,
    own_weight_out,
    sent_weight_out,
    query_out,
    combined_out,
    one_hot_ref,
    sems,
):
    head_index = lax.axis_index("head")
    copies = fetch_weight(slots, head_index, out_weight_hbm, own_weight_out, sems.at[0])
    copies += fetch_weight(slots, head_index ^ 1, out_weight_hbm, sent_weight_out, sems.at[1])
    fill_one_hot(index_ref, one_hot_ref)
    quarter_heads = table_ref.shape[1] // slots
    table_rows = table_ref.shape[2]
    stride = weight_out.shape[1] // table_ref.shape[1]
    stretch_len = weight_out.shape[0] // STRETCHES_DEV
    level = lax.broadcasted_iota(jnp.int32, (levels, table_rows), 0)
    scale = jnp.zeros((levels, table_rows), F32)
    for index in range(levels):
        scale = jnp.where(level == index, level_scale(index, stretch_len), scale)
    tables = []
    for slot in range(slots):
        for spot in range(quarter_heads):
            head = quarter_of(slot, slots) * quarter_heads + spot
            tables.append(table_ref[:, pl.ds(head, 1), :].reshape(levels, table_rows) * scale)
            if stride > levels:
                tables.append(jnp.zeros((stride - levels, table_rows), F32))
    parts = exact_parts(jnp.concatenate(tables, axis=0))
    weight_out[...] = dot_nn(parts, one_hot_ref[...]).T
    local_levels(
        slots, head_dim, 0, query_ref, key_ref, value_ref, cos_ref, sin_ref, bucket_ref,
        weight_out, query_out, combined_out
    )
    for copy in copies:
        copy.wait()


def low_levels(queries, head, weight_ref, heads, low_refs):
    slots = len(low_refs)
    quarter_heads = heads // slots
    stride = weight_ref.shape[1] // heads
    low_bits = low_refs[0].shape[0] // quarter_heads
    first = len(local_plan(STRETCHES_DEV)[-1]) + 1
    shard_index = lax.axis_index("ctx")
    total = None
    for bit in range(low_bits):
        bucket = low_refs[head // quarter_heads][bit * quarter_heads + head % quarter_heads]
        column = head * stride + first + bit
        present = (shard_index >> bit & 1).astype(F32)
        part = weight_ref[:, column : column + 1] * present * dot_nn(queries, bucket)
        total = part if total is None else total + part
    return total


def second_local_kernel(
    head_dim,
    query_ref,
    key_ref,
    value_ref,
    cos_ref,
    sin_ref,
    bucket_ref,
    weight_ref,
    first_query_ref,
    first_combined_ref,
    *refs,
):
    *low_refs, first_combined_out, query_out, combined_out = refs
    heads = bucket_ref.shape[0]
    for head in range(heads // 2):
        cols = slice(head * head_dim, (head + 1) * head_dim)
        first_combined_out[:, cols] = first_combined_ref[:, cols] + low_levels(
            first_query_ref[:, cols], head, weight_ref, heads, low_refs
        )
    local_levels(
        len(low_refs), head_dim, heads // 2, query_ref, key_ref, value_ref, cos_ref, sin_ref, bucket_ref,
        weight_ref, query_out, combined_out, low_refs
    )


def low_kernel(slots, low_bits, *refs):
    parts = [ref[...].astype(F32) for ref in refs[:slots]]
    total_out, *low_outs = refs[slots:]
    quarter_heads = parts[0].shape[0]
    total_out[...] = sum(parts).astype(BF16)
    for by in range(slots):
        for bit in range(low_bits):
            members = [m ^ by for m in range(slots) if m >> bit == 1]
            rows = slice(bit * quarter_heads, (bit + 1) * quarter_heads)
            low_outs[by][rows] = sum(parts[m] for m in members).astype(BF16)


def high_kernel(first_bit, bit_counts, *refs):
    *back_refs, out_ref = refs
    shard_index = lax.axis_index("ctx")
    quarter_heads = back_refs[0].shape[0]
    spot = 0
    level = 0
    for bits in bit_counts:
        radix = 1 << bits
        back = [ref[...].astype(F32) for ref in back_refs[spot : spot + radix - 1]]
        spot += radix - 1
        digit = shard_index >> (first_bit + level) & (radix - 1)
        out_ref[level * quarter_heads : (level + 1) * quarter_heads] = back[0].astype(BF16)
        level += 1
        if bits == 2:
            both = jnp.where(digit == 2, back[0] + back[1], back[1] + back[2])
            out_ref[level * quarter_heads : (level + 1) * quarter_heads] = both.astype(BF16)
            level += 1


def cross_kernel(
    first_slot,
    slots,
    all_slots,
    head_dim,
    levels,
    high_levels,
    combined_ref,
    query_ref,
    weight_ref,
    gain_ref,
    *refs,
):
    *high_refs, hidden_out = refs
    quarter_heads = hidden_out.shape[1] // head_dim // slots
    stride = weight_ref.shape[1] // (all_slots * quarter_heads)
    shard_index = lax.axis_index("ctx")
    first_bit = all_slots.bit_length() - 1
    present = [
        (shard_index >> (first_bit + bit) & 1).astype(F32) for bit in range(high_levels)
    ]
    for slot in range(slots):
        for spot in range(quarter_heads):
            here = slot * quarter_heads + spot
            head = first_slot * quarter_heads + here
            cols = slice(here * head_dim, (here + 1) * head_dim)
            total = combined_ref[:, cols]
            queries = query_ref[:, cols]
            for level in range(high_levels):
                bucket = high_refs[slot][level * quarter_heads + spot]
                column = head * stride + levels - high_levels + level
                weight = weight_ref[:, column : column + 1] * present[level]
                total = total + weight * dot_nn(queries, bucket)
            mean_square = jnp.mean(total * total, axis=-1, keepdims=True)
            source = quarter_of(first_slot + slot, all_slots) * quarter_heads + spot
            gain = gain_ref[pl.ds(source, 1), :]
            normed = total * lax.rsqrt(mean_square + NORM_EPS) * gain
            hidden_out[:, cols] = normed.astype(BF16)


def early_kernel(tile, own_first, own_second, other_first, own_weight, other_weight, out_ref):
    depth = own_first.shape[1]
    for start in range(0, out_ref.shape[1], tile):
        cols = slice(start, start + tile)
        out_ref[:, cols] = (
            dot_nn(own_first[...], own_weight[0:depth, cols])
            + dot_nn(own_second[...], own_weight[depth:, cols])
            + dot_nn(other_first[...], other_weight[0:depth, cols])
        )


def late_kernel(tile, other_second, other_weight, part_ref, out_hbm, out_ref, sems):
    depth = other_second.shape[1]
    copies = []
    for index, start in enumerate(range(0, out_ref.shape[0], tile)):
        rows = slice(start, start + tile)
        total = part_ref[rows, :] + dot_nn(other_second[rows, :], other_weight[depth:, :])
        out_ref[rows, :] = total.astype(BF16)
        copies.append(
            pltpu.make_async_copy(out_ref.at[rows, :], out_hbm.at[rows, :], sems.at[index])
        )
        copies[-1].start()
    for copy in copies:
        copy.wait()


def call(kernel, name, operands, in_spaces, out_shapes, out_spaces, scratch, limit, flops, size):
    return pl.pallas_call(
        kernel,
        in_specs=[pl.BlockSpec(memory_space=space) for space in in_spaces],
        out_specs=[pl.BlockSpec(memory_space=space) for space in out_spaces],
        out_shape=out_shapes,
        scratch_shapes=scratch,
        compiler_params=pltpu.CompilerParams(vmem_limit_bytes=limit),
        cost_estimate=pl.CostEstimate(
            flops=int(flops), bytes_accessed=int(size), transcendentals=0
        ),
        name=name,
    )(*operands)


def local(queries, key_vectors, values, level_table, weight_index, norm_gain, out_weight):
    tok_rows, model_width = queries.shape
    table_rows, heads_here, levels = level_table.shape
    head_dim = model_width // heads_here
    stretch_len = tok_rows // STRETCHES_DEV
    n_ctx = lax.axis_size("ctx")
    n_head = lax.axis_size("head")
    ctx_bits = n_ctx.bit_length() - 1
    group_count = len(bucket_groups())
    low_bits = min(2, ctx_bits)
    high_bits = ctx_bits - low_bits
    slots = 1 << low_bits
    quarter_heads = heads_here // slots
    chunk = slots // 2
    half_width = model_width // 2
    out_cols = out_weight.shape[1] // n_head
    ANY, VMEM = pl.ANY, pltpu.VMEM

    def swap_heads(block):
        return lax.ppermute(block, "head", [(i, i ^ 1) for i in range(n_head)])

    def swap_low(block, by):
        return lax.ppermute(block, "ctx", [(i, i ^ by) for i in range(n_ctx)])

    coarse = tok_rows // FINE
    angles = np.concatenate(
        angle_rows(np.arange(FINE), head_dim)
        + angle_rows(np.arange(coarse) * FINE, head_dim)
        + angle_rows(np.arange(n_ctx) * tok_rows, head_dim)
    )
    head_macs = tok_rows * head_dim * head_dim
    block_bytes = tok_rows * model_width * 2

    def share(count=quarter_heads):
        return VMEM((count, head_dim, head_dim), BF16)

    block = VMEM((tok_rows, model_width), BF16)
    angle_block = VMEM((tok_rows, head_dim), F32)
    moved, moved_values, keys, cosine, sine, local_states, *shares = call(
        functools.partial(state_kernel, slots, head_dim, n_ctx),
        "states",
        (angles, queries, key_vectors, values),
        [ANY] * 4,
        [
            block,
            block,
            block,
            angle_block,
            angle_block,
            VMEM((heads_here, group_count, head_dim, head_dim), BF16),
        ]
        + [share()] * slots,
        [VMEM] * (6 + slots),
        [block, VMEM(angles.shape, F32), pltpu.SemaphoreType.DMA((4, STRETCHES_DEV))],
        FETCH_LIMIT,
        4 * head_macs * heads_here,
        4 * block_bytes,
    )

    parts = [shares[0]] + [swap_low(shares[by], by) for by in range(1, slots)]
    half = VMEM((tok_rows, half_width), BF16)
    half_wide = VMEM((tok_rows, half_width), F32)
    weight_block = VMEM((model_width, out_cols), BF16)
    stride = -(-levels // 8) * 8
    level_block = VMEM((tok_rows, heads_here * stride), F32)
    inputs = (moved, keys, moved_values, cosine, sine, local_states)
    level_weights, own_weight, sent_weight, first_queries, first_combined = call(
        functools.partial(first_local_kernel, slots, head_dim, levels),
        "local_levels_first",
        (weight_index.reshape(1, tok_rows), level_table.transpose(2, 1, 0), out_weight) + inputs,
        [VMEM, VMEM, ANY] + [VMEM] * len(inputs),
        [level_block, weight_block, weight_block, half, half_wide],
        [VMEM] * 5,
        [VMEM((3 * table_rows, tok_rows), BF16), pltpu.SemaphoreType.DMA((2, slots))],
        LOCAL_LIMIT,
        3 * head_macs * heads_here,
        2 * block_bytes,
    )
    parts, inputs, level_weights, sent_weight = lax.optimization_barrier(
        (parts, inputs, level_weights, sent_weight)
    )
    other_block = swap_heads(sent_weight)

    low_count = low_bits * quarter_heads
    high_count = high_bits * quarter_heads
    total, *low_payloads = call(
        functools.partial(low_kernel, slots, low_bits),
        "low_buckets",
        parts,
        [VMEM] * slots,
        [share()] + [share(low_count)] * slots,
        [VMEM] * (1 + slots),
        [],
        SMALL_LIMIT,
        0,
        block_bytes,
    )

    back, bit_counts = [], []
    running = total
    for low in range(low_bits, ctx_bits, 2):
        bits = min(2, ctx_bits - low)
        radix = 1 << bits
        mask = (radix - 1) << low

        def turned(index, by):
            return index & ~mask | (((index >> low) + by) & (radix - 1)) << low

        arrived = [
            lax.ppermute(running, "ctx", [(i, turned(i, by)) for i in range(n_ctx)])
            for by in range(1, radix)
        ]
        back += arrived
        bit_counts.append(bits)
        if low + bits < ctx_bits:
            running = sum(a.astype(F32) for a in [running] + arrived).astype(BF16)

    low_slots = [low_payloads[0]] + [swap_low(low_payloads[by], by) for by in range(1, slots)]
    (high,) = call(
        functools.partial(high_kernel, low_bits, tuple(bit_counts)),
        "high_buckets",
        back,
        [VMEM] * len(back),
        [share(high_count)],
        [VMEM],
        [],
        SMALL_LIMIT,
        0,
        block_bytes,
    )
    high_slots = [swap_low(high, by) for by in range(slots - 1, 0, -1)]
    high_slots = [high] + high_slots[::-1]

    operands = inputs + (level_weights, first_queries, first_combined, *low_slots)
    first_combined, second_queries, second_combined = call(
        functools.partial(second_local_kernel, head_dim),
        "local_levels_second",
        operands,
        [VMEM] * len(operands),
        [half_wide, half, half_wide],
        [VMEM] * 3,
        [],
        SMALL_LIMIT,
        5 * head_macs * heads_here,
        2 * block_bytes,
    )

    gain, second_combined = lax.optimization_barrier((norm_gain, second_combined))
    gain = gain.reshape(heads_here, head_dim)
    hidden = []
    for first, combined, rotated_queries in (
        (0, first_combined, first_queries),
        (chunk, second_combined, second_queries),
    ):
        operands = (
            combined,
            rotated_queries,
            level_weights,
            gain,
            *high_slots[first : first + chunk],
        )
        (piece,) = call(
            functools.partial(
                cross_kernel, first, chunk, slots, head_dim, levels, high_bits
            ),
            "cross_levels",
            operands,
            [VMEM] * len(operands),
            [half],
            [VMEM],
            [],
            SMALL_LIMIT,
            ctx_bits * head_macs * heads_here,
            block_bytes,
        )
        hidden.append(piece)
    other_hidden = [swap_heads(piece) for piece in hidden]

    tile = min(256, out_cols)
    (part,) = call(
        functools.partial(early_kernel, tile),
        "early_projection",
        (hidden[0], hidden[1], other_hidden[0], own_weight, other_block),
        [VMEM] * 5,
        [VMEM((tok_rows, out_cols), F32)],
        [VMEM],
        [],
        SMALL_LIMIT,
        3 * tok_rows * model_width * out_cols,
        2 * block_bytes,
    )
    (mixed_out,) = call(
        functools.partial(late_kernel, tok_rows // STRETCHES_DEV),
        "late_projection",
        (other_hidden[1], other_block, part),
        [VMEM] * 3,
        [jax.ShapeDtypeStruct((tok_rows, out_cols), BF16)],
        [ANY],
        [VMEM((tok_rows, out_cols), BF16), pltpu.SemaphoreType.DMA((STRETCHES_DEV,))],
        SMALL_LIMIT,
        tok_rows * model_width * out_cols,
        2 * block_bytes,
    )
    return mixed_out


def solution(mesh):
    return jax.shard_map(
        local,
        mesh=mesh,
        in_specs=(
            P("ctx", "head"),
            P("ctx", "head"),
            P("ctx", "head"),
            P(None, "head", None),
            P("ctx"),
            P("head"),
            P("head", None),
        ),
        out_specs=P("ctx", "head"),
        check_vma=False,
    )
```
